128 devices in a mesh: pipe: 4 (over x_hi, core), seq: 32 (over x_lo, y, z).
Axes of the slice: x: 4 (x_hi: 2, x_lo: 2; x = x_hi * 2 + x_lo), y: 4, z: 4, core: 2. Of those that a mesh axis runs over, the one named last changes fastest.
Arguments:
- queries: bfloat16 [4, 4096, 4096], P('pipe', 'seq'), may hold values from -11 to 11
- shared_keys: bfloat16 [4096, 512], P('seq', 'pipe'), may hold values from -6 to 6
- shared_values: bfloat16 [4096, 512], P('seq', 'pipe'), may hold values from -6 to 6
- out_grad: bfloat16 [4, 4096, 4096], P('pipe', 'seq'), may hold values from -6 to 6
Outputs:
- query_grad: bfloat16 [4, 4096, 4096], P('pipe', 'seq')
- key_grad: bfloat16 [4096, 512], P('seq', 'pipe')
- value_grad: bfloat16 [4096, 512], P('seq', 'pipe')
The draws below stay inside these ranges and needn't reach their ends.
All inputs are finite; a program needn't handle non-finite values.
Results may differ from the reference program's by a relative error of at most 0.006.
Values may be sent and summed in bfloat16 or wider, within the bound.
A program may use at most 128 MiB of HBM per device.

```python
import math
import jax
import jax.numpy as jnp
from jax import lax

HQ = 32
KVH = 4
DH = 128
SEQ = 4096
SECTIONS = 4


def shared_field(key):
    base_key = jax.random.fold_in(key, 11)
    field = jnp.clip(jax.random.normal(base_key, (SEQ, KVH * DH), jnp.float32), -6.0, 6.0)
    return field


def draw_shared_keys(key, part):
    field = shared_field(key)
    return field.astype(jnp.bfloat16)


def draw_queries(key, part):
    query_key = jax.random.fold_in(key, 23)
    fresh = jnp.clip(jax.random.normal(query_key, (SECTIONS, SEQ, HQ * DH), jnp.float32), -6.0, 6.0)
    return fresh.astype(jnp.bfloat16)


def shard_levels(rng, extent, shards, smallest, high):
    gain, own = 1.0, jax.random.fold_in(rng, 6)
    for position, shards_of in shards:
        heights = jnp.exp(jax.random.uniform(jax.random.fold_in(own, position), (shards_of,), jnp.float32, smallest / len(shards), high / len(shards)))
        gain = gain * jnp.repeat(heights, extent[position] // shards_of).reshape([-1 if axis == position else 1 for axis in range(len(extent))])
    return gain


def normal_values(own_key, shape, scale, most, shards=(), held_as=jnp.bfloat16):
    gain = shard_levels(own_key, shape, shards, -0.22, 0.18) if shards else 1.0
    drawn = jax.random.normal(own_key, shape, jnp.float32) * scale * gain
    return jnp.minimum(jnp.maximum(drawn, -most), most).astype(held_as)


def setup_inputs(seed: int = 0) -> dict:
    key_of = jax.random.split(jax.random.key(seed), 5)
    queries = draw_queries(jax.random.fold_in(key_of[4], 71), 0)
    shared_keys = draw_shared_keys(jax.random.fold_in(key_of[4], 71), 0)
    shared_values = normal_values(key_of[2], (SEQ, KVH * DH), 1.0, 6.0, ((0, 32), (1, 4)))
    out_grad = normal_values(key_of[3], (SECTIONS, SEQ, HQ * DH), 1.0, 6.0, ((0, 4), (1, 32)))
    return {"queries": queries, "shared_keys": shared_keys, "shared_values": shared_values, "out_grad": out_grad}


def head_grads(query_head, key_head, value_head, grad_head):
    scale = 1.0 / math.sqrt(DH)
    scores = jnp.dot(query_head, key_head.T, preferred_element_type=jnp.float32) * scale
    positions = jnp.arange(SEQ, dtype=jnp.int32)
    visible = positions[:, None] >= positions[None, :]
    scores = jnp.where(visible, scores, jnp.float32(-1e+30))
    top = lax.optimization_barrier(jnp.max(scores, axis=1, keepdims=True))
    weights = jnp.where(visible, jnp.exp(scores - top), jnp.float32(0.0))
    probs = weights / lax.optimization_barrier(jnp.sum(weights, axis=1, keepdims=True))
    prob_grad = jnp.dot(grad_head, value_head.T, preferred_element_type=jnp.float32)
    row_dot = lax.optimization_barrier(jnp.sum(probs * prob_grad, axis=1, keepdims=True))
    score_grad = probs * (prob_grad - row_dot)
    probs_low = probs.astype(jnp.bfloat16)
    score_low = score_grad.astype(jnp.bfloat16)
    value_grad = jnp.dot(probs_low.T, grad_head, preferred_element_type=jnp.float32)
    key_grad = jnp.dot(score_low.T, query_head, preferred_element_type=jnp.float32) * scale
    query_grad = jnp.dot(score_low, key_head, preferred_element_type=jnp.float32) * scale
    return (query_grad, key_grad, value_grad)

def section_grads(section_queries, section_cotangent, shared_keys, shared_values):
    group_size = HQ // KVH

    def one_head(head):
        kv_index = head // group_size
        query_head = lax.dynamic_slice_in_dim(section_queries, head * DH, DH, 1)
        grad_head = lax.dynamic_slice_in_dim(section_cotangent, head * DH, DH, 1)
        key_head = lax.dynamic_slice_in_dim(shared_keys, kv_index * DH, DH, 1)
        value_head = lax.dynamic_slice_in_dim(shared_values, kv_index * DH, DH, 1)
        return head_grads(query_head, key_head, value_head, grad_head)
    query_parts, key_parts, value_parts = lax.map(one_head, jnp.arange(HQ, dtype=jnp.int32))
    query_grad = query_parts.transpose(1, 0, 2).reshape(SEQ, HQ * DH)
    key_sum = key_parts.reshape(KVH, group_size, SEQ, DH).sum(axis=1).transpose(1, 0, 2).reshape(SEQ, KVH * DH)
    value_sum = value_parts.reshape(KVH, group_size, SEQ, DH).sum(axis=1).transpose(1, 0, 2).reshape(SEQ, KVH * DH)
    return (query_grad, key_sum, value_sum)

def reference(queries, shared_keys, shared_values, out_grad):
    key_total = jnp.zeros((SEQ, KVH * DH), jnp.float32)
    value_total = jnp.zeros((SEQ, KVH * DH), jnp.float32)
    query_list = []
    for section in range(SECTIONS):
        query_grad, key_sum, value_sum = section_grads(queries[section], out_grad[section], shared_keys, shared_values)
        query_list.append(query_grad.astype(jnp.bfloat16))
        key_total = key_total + key_sum
        value_total = value_total + value_sum
    return (jnp.stack(query_list, axis=0), key_total.astype(jnp.bfloat16), value_total.astype(jnp.bfloat16))
```

```python
import functools
import math

import jax
import jax.numpy as jnp
from jax import lax
from jax.experimental import pallas as pl
from jax.experimental.pallas import tpu as pltpu
from jax.sharding import PartitionSpec as P

DH = 128
TOK = 128
CH = 256
SCALE = 1.0 / math.sqrt(DH)
EXPO = math.log2(math.e) / math.sqrt(DH)
f32, bf16 = jnp.float32, jnp.bfloat16
NN = (((1,), (0,)), ((), ()))


def dot(a, b):
    return lax.dot_general(a, b, NN, preferred_element_type=f32)


def lanes(start, size):
    return pl.ds(pl.multiple_of(start, 128), size)


def kernel(
    q_in, k_in, v_in, g_in,
    dq_out, dk_out, dv_out,
    q_s, g_s, dq_s, kv, q_t, g_t, k_t, acc, dkv,
    m8, l8, d8, top, rdot,
    st1, rc1, st2, rc2, red, st3, rc3, st4, rc4, fin, rcx,
    ex_send, ex_recv, loc, a_send, a_recv, ag_send, ag_recv,
    rs_send, rs_recv, x_send, x_recv, dq_send, dq_recv,
):
    pipe = lax.axis_index("pipe")
    seq = lax.axis_index("seq")
    x_hi, core = pipe // 2, pipe % 2
    x_lo, y, z = seq // 16, (seq // 4) % 4, seq % 4
    head = 2 * x_lo + core

    def dev(x_hi_, core_, x_lo_, y_, z_):
        return {"pipe": x_hi_ * 2 + core_, "seq": x_lo_ * 16 + y_ * 4 + z_}

    def remote(src, dst, send, recv, to):
        return pltpu.make_async_remote_copy(
            src_ref=src, dst_ref=dst, send_sem=send, recv_sem=recv,
            device_id=to, device_id_type=pl.DeviceIdType.MESH,
        )

    mates = [
        dev(x_hi, 1 - core, x_lo, y, z),
        dev(x_hi, core, 1 - x_lo, 3 - y, 3 - z),
        dev(x_hi, 1 - core, 1 - x_lo, 3 - y, 3 - z),
    ]
    y_up, y_dn = dev(x_hi, core, x_lo, (y + 1) % 4, z), dev(x_hi, core, x_lo, (y + 3) % 4, z)
    z_up, z_dn = dev(x_hi, core, x_lo, y, (z + 1) % 4), dev(x_hi, core, x_lo, y, (z + 3) % 4)
    ring = ((y_up, y_dn), (z_up, z_dn))

    def x_to(t):
        return dev(t, core, x_hi, y, z)

    def x_from(s):
        return dev(x_lo, core, s, y, z)

    barrier = pltpu.get_barrier_semaphore()
    for peer in mates + [y_up, y_dn, z_up, z_dn]:
        pl.semaphore_signal(barrier, inc=1, device_id=peer, device_id_type=pl.DeviceIdType.MESH)
    for t in range(2):
        @pl.when(jnp.logical_not(jnp.logical_and(t == x_hi, x_lo == x_hi)))
        def _():
            pl.semaphore_signal(barrier, inc=1, device_id=x_to(t), device_id_type=pl.DeviceIdType.MESH)

        @pl.when(jnp.logical_not(jnp.logical_and(x_lo == x_hi, t == x_lo)))
        def _():
            pl.semaphore_signal(barrier, inc=1, device_id=x_from(t), device_id_type=pl.DeviceIdType.MESH)

    @pl.when(x_hi == x_lo)
    def _():
        pl.semaphore_wait(barrier, 9)

    @pl.when(x_hi != x_lo)
    def _():
        pl.semaphore_wait(barrier, 11)

    def a_copies(t):
        to_self = jnp.logical_and(t == x_hi, x_lo == x_hi)
        pairs = []
        for i, src in enumerate((k_in, v_in)):
            dst = kv.at[i, x_lo, y, z]
            pairs.append((
                pltpu.make_async_copy(src, dst, a_recv.at[i, x_lo]),
                remote(src, dst, a_send.at[i, t], a_recv.at[i, x_lo], x_to(t)),
            ))
        return to_self, pairs

    for t in range(2):
        to_self, pairs = a_copies(t)
        for local, away in pairs:
            @pl.when(to_self)
            def _(local=local):
                local.start()

            @pl.when(jnp.logical_not(to_self))
            def _(away=away):
                away.start()

    ex = []
    for n, (c_t, flip) in enumerate(((1 - core, 0), (core, 1), (1 - core, 1))):
        x_t = (1 - x_lo) if flip else x_lo
        cols = lanes((2 * x_t + c_t) * 1024, 1024)
        slot = 2 * flip + core
        for i, (src, dst) in enumerate(((q_in, q_s), (g_in, g_s))):
            ex.append(remote(src.at[:, cols], dst.at[slot], ex_send.at[i, n], ex_recv.at[i, n], mates[n]))
    for copy in ex:
        copy.start()
    own_cols = lanes(head * 1024, 1024)
    own = [
        pltpu.make_async_copy(q_in.at[:, own_cols], q_s.at[core], loc.at[0]),
        pltpu.make_async_copy(g_in.at[:, own_cols], g_s.at[core], loc.at[1]),
    ]
    for copy in own:
        copy.start()

    dkv[...] = jnp.zeros_like(dkv)
    acc[...] = jnp.zeros_like(acc)
    m8[...] = jnp.full_like(m8, -1e30)
    l8[...] = jnp.zeros_like(l8)
    d8[...] = jnp.zeros_like(d8)

    for i in range(2):
        for s in range(2):
            pltpu.make_async_copy(k_in, kv.at[i, s, y, z], a_recv.at[i, s]).wait()

    def one(h, yy, zz, first):
        return kv.at[:, h, yy, zz] if first else (kv.at[:, 0, :, zz] if h == 0 else kv.at[:, 1, yy, :])

    def part(i, h, yy, zz, first):
        return kv.at[i, h, yy, zz] if first else (kv.at[i, 0, :, zz] if h == 0 else kv.at[i, 1, yy, :])

    sent = []
    for stage in range(2):
        steps = []
        for h in range(2):
            along_y = (h == 0) == (stage == 0)
            up, dn = ring[0] if along_y else ring[1]
            here = one(h, y, z, stage == 0)
            steps.append(remote(here, here, ag_send.at[stage, h, 0], ag_recv.at[stage, h, 0], up))
            steps.append(remote(here, here, ag_send.at[stage, h, 1], ag_recv.at[stage, h, 1], dn))
        for copy in steps:
            copy.start()
        for copy in steps:
            copy.wait_recv()
        more = []
        for h in range(2):
            along_y = (h == 0) == (stage == 0)
            up, dn = ring[0] if along_y else ring[1]
            if along_y:
                low, high = part(0, h, (y + 3) % 4, z, stage == 0), part(1, h, (y + 1) % 4, z, stage == 0)
            else:
                low, high = part(0, h, y, (z + 3) % 4, stage == 0), part(1, h, y, (z + 1) % 4, stage == 0)
            more.append(remote(low, low, ag_send.at[stage, h, 2], ag_recv.at[stage, h, 2], up))
            more.append(remote(high, high, ag_send.at[stage, h, 3], ag_recv.at[stage, h, 3], dn))
        for copy in more:
            copy.start()
        for copy in more:
            copy.wait_recv()
        sent += steps + more

    for copy in own:
        copy.wait()
    for copy in ex:
        copy.wait_recv()

    def tile2(ref, i):
        s, n = i // 4, i % 4
        return jnp.concatenate(
            [ref[s, :, lanes(n * 256, 128)], ref[s, :, lanes(n * 256 + 128, 128)]], axis=0
        )

    def prep(i, carry):
        cols = lanes(i * 256, 256)
        q_t[:, cols] = tile2(q_s, i).T
        g_t[:, cols] = tile2(g_s, i).T
        return carry

    lax.fori_loop(0, 16, prep, 0)

    def keys(i, kc):
        return kv[i, kc // 8, (kc // 2) % 4, pl.ds(2 * (kc % 2), 2)].reshape(CH, DH)

    def prep_k(kc, carry):
        k_t[:, lanes(kc * CH, CH)] = keys(0, kc).T
        return carry

    lax.fori_loop(0, 16, prep_k, 0)

    def visible(pos, kc):
        key_pos = kc * CH + lax.broadcasted_iota(jnp.int32, (CH, 256), 0)
        query_pos = pos * TOK + (lax.broadcasted_iota(jnp.int32, (CH, 256), 1) & 127)
        return key_pos <= query_pos

    def stats(pos, kc, i, masked):
        cols = lanes(i * 256, 256)
        s = dot(keys(0, kc), q_t[:, cols])
        dp = dot(keys(1, kc), g_t[:, cols])
        if masked:
            s = jnp.where(visible(pos, kc), s, -1e30)
        s = s.reshape(CH // 8, 8, 256)
        dp = dp.reshape(CH // 8, 8, 256)
        old = m8[:, cols]
        new = jnp.maximum(old, jnp.max(s, axis=0))
        w = jnp.exp2((s - new) * EXPO)
        shrink = jnp.exp2((old - new) * EXPO)
        m8[:, cols] = new
        l8[:, cols] = l8[:, cols] * shrink + jnp.sum(w, axis=0)
        d8[:, cols] = d8[:, cols] * shrink + jnp.sum(w * dp, axis=0)

    def grads(pos, kc, i, masked):
        cols = lanes(i * 256, 256)
        at = (kc // 8, (kc // 2) % 4, pl.ds(2 * (kc % 2), 2))
        s = dot(keys(0, kc), q_t[:, cols])
        dp = dot(keys(1, kc), g_t[:, cols])
        p = jnp.exp2(s * EXPO - top[:, cols])
        if masked:
            p = jnp.where(visible(pos, kc), p, 0.0)
        ds = p * (dp - rdot[:, cols])
        p_low, ds_low = p.astype(bf16), ds.astype(bf16)
        dkv[(1,) + at] += dot(p_low, tile2(g_s, i)).reshape(2, 128, 128)
        dkv[(0,) + at] += dot(ds_low, tile2(q_s, i)).reshape(2, 128, 128)
        acc[:, cols] += dot(k_t[:, lanes(kc * CH, CH)], ds_low)

    positions = (seq, 31 - seq)

    def sweep(fn):
        for blk in range(2):
            pos = positions[blk]

            def chunk(kc, carry, masked=False, pos=pos, blk=blk):
                for i in range(8):
                    fn(pos, kc, blk * 8 + i, masked)
                return carry

            lax.fori_loop(0, pos // 2, chunk, 0)
            chunk(pos // 2, 0, True)

    sweep(stats)
    high = jnp.max(m8[...], axis=0, keepdims=True)
    fold = jnp.exp2((m8[...] - high) * EXPO)
    total = jnp.sum(l8[...] * fold, axis=0, keepdims=True)
    top[...] = high * EXPO + jnp.log2(total)
    rdot[...] = jnp.sum(d8[...] * fold, axis=0, keepdims=True) / total
    sweep(grads)

    def finish(i, carry):
        s, n = i // 4, i % 4
        t = (acc[:, lanes(i * 256, 256)] * SCALE).T.astype(bf16)
        dq_s[s, :, lanes(n * 256, 128)] = t[:128]
        dq_s[s, :, lanes(n * 256 + 128, 128)] = t[128:]
        return carry

    lax.fori_loop(0, 16, finish, 0)

    back = []
    for n, (c_t, flip) in enumerate(((1 - core, 0), (core, 1), (1 - core, 1))):
        back.append(remote(
            dq_s.at[2 * flip + c_t], dq_out.at[:, own_cols], dq_send.at[n], dq_recv.at[n], mates[n]
        ))
    for copy in back:
        copy.start()
    mine = pltpu.make_async_copy(dq_s.at[core], dq_out.at[:, own_cols], loc.at[2])
    mine.start()

    def part_of(h, i, d):
        return dkv[i, 0, :, d] if h == 0 else dkv[i, 1, d, :]

    spots = (z, y)
    rings = ((z_up, z_dn), (y_up, y_dn))
    first = []
    for h in range(2):
        spot, (up, dn) = spots[h], rings[h]
        far = (spot + 2) % 4
        st1[h, 0] = part_of(h, 0, far).astype(bf16)
        st1[h, 1] = part_of(h, 1, far).astype(bf16)
        first.append(remote(st1.at[h, 0], rc1.at[h, 0], rs_send.at[0, h, 0], rs_recv.at[0, h, 0], dn))
        first.append(remote(st1.at[h, 1], rc1.at[h, 1], rs_send.at[0, h, 1], rs_recv.at[0, h, 1], up))
        first[-2].start()
        first[-1].start()
    for h in range(2):
        spot = spots[h]
        st2[h, 0, 1] = part_of(h, 1, (spot + 3) % 4).astype(bf16)
        st2[h, 1, 0] = part_of(h, 0, (spot + 1) % 4).astype(bf16)
    second = []
    for h in range(2):
        spot, (up, dn) = spots[h], rings[h]
        first[2 * h].wait_recv()
        st2[h, 0, 0] = (part_of(h, 0, (spot + 3) % 4) + rc1[h, 0].astype(f32)).astype(bf16)
        second.append(remote(st2.at[h, 0], rc2.at[h, 0], rs_send.at[1, h, 0], rs_recv.at[1, h, 0], dn))
        second[-1].start()
        first[2 * h + 1].wait_recv()
        st2[h, 1, 1] = (part_of(h, 1, (spot + 1) % 4) + rc1[h, 1].astype(f32)).astype(bf16)
        second.append(remote(st2.at[h, 1], rc2.at[h, 1], rs_send.at[1, h, 1], rs_recv.at[1, h, 1], up))
        second[-1].start()
    for h in range(2):
        second[2 * h].wait_recv()
        second[2 * h + 1].wait_recv()
        for i in range(2):
            red[h, i] = part_of(h, i, spots[h]) + rc2[h, 0, i].astype(f32) + rc2[h, 1, i].astype(f32)

    third, fourth = [], []
    for h in range(2):
        spot, (up, dn) = spots[1 - h], rings[1 - h]
        far = (spot + 2) % 4
        st3[h, 0] = red[h, 0, far]
        st3[h, 1] = red[h, 1, far]
        third.append(remote(st3.at[h, 0], rc3.at[h, 0], rs_send.at[2, h, 0], rs_recv.at[2, h, 0], dn))
        third.append(remote(st3.at[h, 1], rc3.at[h, 1], rs_send.at[2, h, 1], rs_recv.at[2, h, 1], up))
        third[-2].start()
        third[-1].start()
        st4[h, 0, 1] = red[h, 1, (spot + 3) % 4]
        st4[h, 1, 0] = red[h, 0, (spot + 1) % 4]
    for h in range(2):
        spot, (up, dn) = spots[1 - h], rings[1 - h]
        third[2 * h].wait_recv()
        st4[h, 0, 0] = red[h, 0, (spot + 3) % 4] + rc3[h, 0]
        fourth.append(remote(st4.at[h, 0], rc4.at[h, 0], rs_send.at[3, h, 0], rs_recv.at[3, h, 0], dn))
        fourth[-1].start()
        third[2 * h + 1].wait_recv()
        st4[h, 1, 1] = red[h, 1, (spot + 1) % 4] + rc3[h, 1]
        fourth.append(remote(st4.at[h, 1], rc4.at[h, 1], rs_send.at[3, h, 1], rs_recv.at[3, h, 1], up))
        fourth[-1].start()

    def x_copies(h):
        to_self = jnp.logical_and(x_hi == x_lo, h == x_lo)
        local = pltpu.make_async_copy(fin.at[h], rcx.at[x_hi], x_recv.at[x_hi])
        away = remote(fin.at[h], rcx.at[x_hi], x_send.at[h], x_recv.at[x_hi], x_from(h))
        return to_self, local, away

    for h in range(2):
        fourth[2 * h].wait_recv()
        fourth[2 * h + 1].wait_recv()
        for i in range(2):
            fin[h, i] = red[h, i, spots[1 - h]] + rc4[h, 0, i] + rc4[h, 1, i]
        to_self, local, away = x_copies(h)

        @pl.when(to_self)
        def _(local=local):
            local.start()

        @pl.when(jnp.logical_not(to_self))
        def _(away=away):
            away.start()

    for s in range(2):
        pltpu.make_async_copy(fin.at[0], rcx.at[s], x_recv.at[s]).wait()
    dk_out[...] = ((rcx[0, 0] + rcx[1, 0]) * SCALE).astype(bf16)
    dv_out[...] = (rcx[0, 1] + rcx[1, 1]).astype(bf16)

    mine.wait()
    for copy in back:
        copy.wait()
    for copy in ex + sent + first + second + third + fourth:
        copy.wait_send()
    for t in range(2):
        to_self, pairs = a_copies(t)
        for _, away in pairs:
            @pl.when(jnp.logical_not(to_self))
            def _(away=away):
                away.wait_send()

        to_self, _, away = x_copies(t)

        @pl.when(jnp.logical_not(to_self))
        def _(away=away):
            away.wait_send()


def body(queries, shared_keys, shared_values, out_grad):
    any_, vmem = pl.BlockSpec(memory_space=pl.ANY), pl.BlockSpec(memory_space=pltpu.VMEM)
    dma = pltpu.SemaphoreType.DMA
    big, small = (2, 2, 4, 128, 128), (2, 2, 2, 128, 128)
    dq, dk, dv = pl.pallas_call(
        kernel,
        out_shape=(
            jax.ShapeDtypeStruct((128, 4096), bf16),
            jax.ShapeDtypeStruct((128, 128), bf16),
            jax.ShapeDtypeStruct((128, 128), bf16),
        ),
        in_specs=[any_] * 4,
        out_specs=(any_, vmem, vmem),
        scratch_shapes=[
            pltpu.VMEM((4, 128, 1024), bf16),
            pltpu.VMEM((4, 128, 1024), bf16),
            pltpu.VMEM((4, 128, 1024), bf16),
            pltpu.VMEM((2, 2, 4, 4, 128, 128), bf16),
            pltpu.VMEM((128, 4096), bf16),
            pltpu.VMEM((128, 4096), bf16),
            pltpu.VMEM((128, 4096), bf16),
            pltpu.VMEM((128, 4096), f32),
            pltpu.VMEM((2, 2, 4, 4, 128, 128), f32),
            pltpu.VMEM((8, 4096), f32),
            pltpu.VMEM((8, 4096), f32),
            pltpu.VMEM((8, 4096), f32),
            pltpu.VMEM((1, 4096), f32),
            pltpu.VMEM((1, 4096), f32),
            pltpu.VMEM(big, bf16),
            pltpu.VMEM(big, bf16),
            pltpu.VMEM((2,) + big, bf16),
            pltpu.VMEM((2,) + big, bf16),
            pltpu.VMEM(big, f32),
            pltpu.VMEM((2, 2, 128, 128), f32),
            pltpu.VMEM((2, 2, 128, 128), f32),
            pltpu.VMEM(small, f32),
            pltpu.VMEM(small, f32),
            pltpu.VMEM((2, 2, 128, 128), f32),
            pltpu.VMEM((2, 2, 128, 128), f32),
            dma((2, 3)), dma((2, 3)), dma((3,)),
            dma((2, 2)), dma((2, 2)),
            dma((2, 2, 4)), dma((2, 2, 4)),
            dma((4, 2, 2)), dma((4, 2, 2)),
            dma((2,)), dma((2,)),
            dma((3,)), dma((3,)),
        ],
        compiler_params=pltpu.CompilerParams(
            collective_id=0, has_side_effects=True, vmem_limit_bytes=56 * 2**20
        ),
        cost_estimate=pl.CostEstimate(flops=16 * 10**9, bytes_accessed=4 * 2**20, transcendentals=18 * 10**6),
    )(queries[0], shared_keys, shared_values, out_grad[0])
    return dq[None], dk, dv


def solution(mesh):
    return jax.shard_map(
        body,
        mesh=mesh,
        in_specs=(P("pipe", "seq", None), P("seq", "pipe"), P("seq", "pipe"), P("pipe", "seq", None)),
        out_specs=(P("pipe", "seq", None), P("seq", "pipe"), P("seq", "pipe")),
        check_vma=False,
    )
```

```python
import functools
import math

import jax
import jax.numpy as jnp
from jax import lax
from jax.experimental import pallas as pl
from jax.experimental.pallas import tpu as pltpu
from jax.sharding import PartitionSpec as P

DH = 128
TOK = 128
CH = 256
SCALE = 1.0 / math.sqrt(DH)
EXPO = math.log2(math.e) / math.sqrt(DH)
f32, bf16 = jnp.float32, jnp.bfloat16
NN = (((1,), (0,)), ((), ()))


def dot(a, b):
    return lax.dot_general(a, b, NN, preferred_element_type=f32)


def lanes(start, size):
    return pl.ds(pl.multiple_of(start, 128), size)


def kernel(
    q_in, k_in, v_in, g_in,
    dq_out, dk_out, dv_out,
    q_s, g_s, dq_s, kv, q_t, g_t, k_t, acc, dkv,
    m8, l8, d8, top, rdot,
    st1, rc1, st2, rc2, red, st3, rc3, st4, rc4, fin, rcx,
    ex_send, ex_recv, loc, a_send, a_recv, ag_send, ag_recv,
    rs_send, rs_recv, x_send, x_recv, dq_send, dq_recv,
):
    pipe = lax.axis_index("pipe")
    seq = lax.axis_index("seq")
    x_hi, core = pipe // 2, pipe % 2
    x_lo, y, z = seq // 16, (seq // 4) % 4, seq % 4
    head = 2 * x_lo + core

    def dev(x_hi_, core_, x_lo_, y_, z_):
        return {"pipe": x_hi_ * 2 + core_, "seq": x_lo_ * 16 + y_ * 4 + z_}

    def remote(src, dst, send, recv, to):
        return pltpu.make_async_remote_copy(
            src_ref=src, dst_ref=dst, send_sem=send, recv_sem=recv,
            device_id=to, device_id_type=pl.DeviceIdType.MESH,
        )

    mates = [
        dev(x_hi, 1 - core, x_lo, y, z),
        dev(x_hi, core, 1 - x_lo, 3 - y, 3 - z),
        dev(x_hi, 1 - core, 1 - x_lo, 3 - y, 3 - z),
    ]
    y_up, y_dn = dev(x_hi, core, x_lo, (y + 1) % 4, z), dev(x_hi, core, x_lo, (y + 3) % 4, z)
    z_up, z_dn = dev(x_hi, core, x_lo, y, (z + 1) % 4), dev(x_hi, core, x_lo, y, (z + 3) % 4)
    ring = ((y_up, y_dn), (z_up, z_dn))

    def x_to(t):
        return dev(t, core, x_hi, y, z)

    def x_from(s):
        return dev(x_lo, core, s, y, z)

    barrier = pltpu.get_barrier_semaphore()
    for peer in mates + [y_up, y_dn, z_up, z_dn]:
        pl.semaphore_signal(barrier, inc=1, device_id=peer, device_id_type=pl.DeviceIdType.MESH)
    for t in range(2):
        @pl.when(jnp.logical_not(jnp.logical_and(t == x_hi, x_lo == x_hi)))
        def _():
            pl.semaphore_signal(barrier, inc=1, device_id=x_to(t), device_id_type=pl.DeviceIdType.MESH)

        @pl.when(jnp.logical_not(jnp.logical_and(x_lo == x_hi, t == x_lo)))
        def _():
            pl.semaphore_signal(barrier, inc=1, device_id=x_from(t), device_id_type=pl.DeviceIdType.MESH)

    own_cols = lanes(head * 1024, 1024)
    own = [
        pltpu.make_async_copy(q_in.at[:, own_cols], q_s.at[core], loc.at[0]),
        pltpu.make_async_copy(g_in.at[:, own_cols], g_s.at[core], loc.at[1]),
    ]
    for copy in own:
        copy.start()

    def clear(i, carry):
        dkv[i // 8, (i // 4) % 2, i % 4] = jnp.zeros((4, 128, 128), f32)
        return carry

    lax.fori_loop(0, 16, clear, 0)
    acc[...] = jnp.zeros_like(acc)
    m8[...] = jnp.full_like(m8, -1e30)
    l8[...] = jnp.zeros_like(l8)
    d8[...] = jnp.zeros_like(d8)

    def tile2(ref, i):
        s, n = i // 4, i % 4
        return jnp.concatenate(
            [ref[s, :, lanes(n * 256, 128)], ref[s, :, lanes(n * 256 + 128, 128)]], axis=0
        )

    def prep(i, carry=0):
        cols = lanes(i * 256, 256)
        q_t[:, cols] = tile2(q_s, i).T
        g_t[:, cols] = tile2(g_s, i).T
        return carry

    for copy in own:
        copy.wait()
    lax.fori_loop(0, 4, lambda n, carry: prep(core * 4 + n), 0)

    @pl.when(x_hi == x_lo)
    def _():
        pl.semaphore_wait(barrier, 9)

    @pl.when(x_hi != x_lo)
    def _():
        pl.semaphore_wait(barrier, 11)

    def a_copies(t):
        to_self = jnp.logical_and(t == x_hi, x_lo == x_hi)
        pairs = []
        for i, src in enumerate((k_in, v_in)):
            dst = kv.at[i, x_lo, y, z]
            pairs.append((
                pltpu.make_async_copy(src, dst, a_recv.at[i, x_lo]),
                remote(src, dst, a_send.at[i, t], a_recv.at[i, x_lo], x_to(t)),
            ))
        return to_self, pairs

    for t in range(2):
        to_self, pairs = a_copies(t)
        for local, away in pairs:
            @pl.when(to_self)
            def _(local=local):
                local.start()

            @pl.when(jnp.logical_not(to_self))
            def _(away=away):
                away.start()

    def exchange(n, half):
        c_t, flip = ((1 - core, 0), (core, 1), (1 - core, 1))[n]
        x_t = (1 - x_lo) if flip else x_lo
        cols = lanes((2 * x_t + c_t) * 1024 + half * 512, 512)
        there = lanes(half * 512, 512)
        slot = 2 * flip + core
        return [
            remote(src.at[:, cols], dst.at[slot, :, there], ex_send.at[i, n, half], ex_recv.at[i, n, half], mates[n])
            for i, (src, dst) in enumerate(((q_in, q_s), (g_in, g_s)))
        ]

    ex = [[exchange(n, half) for half in range(2)] for n in range(3)]
    for half in range(2):
        for copy in ex[0][half]:
            copy.start()

    for i in range(2):
        for s in range(2):
            pltpu.make_async_copy(k_in, kv.at[i, s, y, z], a_recv.at[i, s]).wait()

    def one(h, yy, zz, first):
        return kv.at[:, h, yy, zz] if first else (kv.at[:, 0, :, zz] if h == 0 else kv.at[:, 1, yy, :])

    def part(i, h, yy, zz, first):
        return kv.at[i, h, yy, zz] if first else (kv.at[i, 0, :, zz] if h == 0 else kv.at[i, 1, yy, :])

    def near(stage):
        steps = []
        for h in range(2):
            along_y = (h == 0) == (stage == 0)
            up, dn = ring[0] if along_y else ring[1]
            here = one(h, y, z, stage == 0)
            steps.append(remote(here, here, ag_send.at[stage, h, 0], ag_recv.at[stage, h, 0], up))
            steps.append(remote(here, here, ag_send.at[stage, h, 1], ag_recv.at[stage, h, 1], dn))
        return steps

    def onward(stage):
        steps = []
        for h in range(2):
            along_y = (h == 0) == (stage == 0)
            up, dn = ring[0] if along_y else ring[1]
            if along_y:
                low, high = part(0, h, (y + 3) % 4, z, stage == 0), part(1, h, (y + 1) % 4, z, stage == 0)
            else:
                low, high = part(0, h, y, (z + 3) % 4, stage == 0), part(1, h, y, (z + 1) % 4, stage == 0)
            steps.append(remote(low, low, ag_send.at[stage, h, 2], ag_recv.at[stage, h, 2], up))
            steps.append(remote(high, high, ag_send.at[stage, h, 3], ag_recv.at[stage, h, 3], dn))
        return steps

    near0, onward0, near1, onward1 = near(0), onward(0), near(1), onward(1)
    for copy in near0:
        copy.start()
    for n in (1, 2):
        for copy in ex[n][0]:
            copy.start()
    for copy in near0:
        copy.wait_recv()
    for copy in onward0:
        copy.start()
    for half in range(2):
        for copy in ex[0][half]:
            copy.wait_recv()
    lax.fori_loop(0, 4, lambda n, carry: prep((1 - core) * 4 + n), 0)
    for copy in onward0:
        copy.wait_recv()
    for copy in near1:
        copy.start()
    for n in (1, 2):
        for copy in ex[n][1]:
            copy.start()

    def keys(i, kc):
        return kv[i, kc // 8, (kc // 2) % 4, pl.ds(2 * (kc % 2), 2)].reshape(CH, DH)

    def visible(pos, kc):
        key_pos = kc * CH + lax.broadcasted_iota(jnp.int32, (CH, 256), 0)
        query_pos = pos * TOK + (lax.broadcasted_iota(jnp.int32, (CH, 256), 1) & 127)
        return key_pos <= query_pos

    def stats(pos, kc, i, masked):
        cols = lanes(i * 256, 256)
        s = dot(keys(0, kc), q_t[:, cols])
        dp = dot(keys(1, kc), g_t[:, cols])
        if masked:
            s = jnp.where(visible(pos, kc), s, -1e30)
        s = s.reshape(CH // 8, 8, 256)
        dp = dp.reshape(CH // 8, 8, 256)
        old = m8[:, cols]
        new = jnp.maximum(old, jnp.max(s, axis=0))
        w = jnp.exp2((s - new) * EXPO)
        shrink = jnp.exp2((old - new) * EXPO)
        m8[:, cols] = new
        l8[:, cols] = l8[:, cols] * shrink + jnp.sum(w, axis=0)
        d8[:, cols] = d8[:, cols] * shrink + jnp.sum(w * dp, axis=0)

    def grads(pos, kc, i, masked):
        cols = lanes(i * 256, 256)
        at = (kc // 8, (kc // 2) % 4, pl.ds(2 * (kc % 2), 2))
        s = dot(keys(0, kc), q_t[:, cols])
        dp = dot(keys(1, kc), g_t[:, cols])
        p = jnp.exp2(s * EXPO - top[:, cols])
        if masked:
            p = jnp.where(visible(pos, kc), p, 0.0)
        ds = p * (dp - rdot[:, cols])
        p_low, ds_low = p.astype(bf16), ds.astype(bf16)
        dkv[(1,) + at] += dot(p_low, tile2(g_s, i)).reshape(2, 128, 128)
        dkv[(0,) + at] += dot(ds_low, tile2(q_s, i)).reshape(2, 128, 128)
        acc[:, cols] += dot(k_t[:, lanes(kc * CH, CH)], ds_low)

    positions = (seq, 31 - seq)

    def chunk(fn, blk, kc, tiles):
        pos = positions[blk]

        @pl.when(kc < pos // 2)
        def _():
            for i in tiles:
                fn(pos, kc, i, False)

        @pl.when(kc == pos // 2)
        def _():
            for i in tiles:
                fn(pos, kc, i, True)

    def near_rows(o, carry):
        @pl.when(o == 2)
        def _():
            for copy in near1:
                copy.wait_recv()
            for copy in onward1:
                copy.start()

        @pl.when(o == 6)
        def _():
            for copy in onward1:
                copy.wait_recv()

        late, r = o // 8, o // 2
        turn = r + r // 2 - 2 * (r // 3)
        kc = (1 - late) * (8 + ((y + turn) % 4) * 2 + o % 2) + late * (o - 8)
        chunk(stats, 0, kc, range(8))
        return carry

    lax.fori_loop(0, 16, near_rows, 0)

    def far_rows(half, carry):
        for n in (1, 2):
            for i in range(2):
                pltpu.make_async_copy(
                    q_s.at[0, :, lanes(0, 512)], q_s.at[0, :, lanes(0, 512)], ex_recv.at[i, n, half]
                ).wait()
        tiles = [8 + 2 * half, 9 + 2 * half, 12 + 2 * half, 13 + 2 * half]
        for i in tiles:
            prep(i)
        pos = positions[1]

        def full(kc, carry):
            for i in tiles:
                stats(pos, kc, i, False)
            return carry

        lax.fori_loop(0, pos // 2, full, 0)
        for i in tiles:
            stats(pos, pos // 2, i, True)
        return carry

    lax.fori_loop(0, 2, far_rows, 0)

    def prep_k(kc, carry):
        k_t[:, lanes(kc * CH, CH)] = keys(0, kc).T
        return carry

    lax.fori_loop(0, 16, prep_k, 0)
    high = jnp.max(m8[...], axis=0, keepdims=True)
    fold = jnp.exp2((m8[...] - high) * EXPO)
    total = jnp.sum(l8[...] * fold, axis=0, keepdims=True)
    top[...] = high * EXPO + jnp.log2(total)
    rdot[...] = jnp.sum(d8[...] * fold, axis=0, keepdims=True) / total

    def part_of(h, i, d):
        return dkv[i, 0, :, d] if h == 0 else dkv[i, 1, d, :]

    spots = (z, y)
    rings = ((z_up, z_dn), (y_up, y_dn))
    first, second, third, fourth = [], [], [], []
    for h in range(2):
        up, dn = rings[h]
        first.append(remote(st1.at[h, 0], rc1.at[h, 0], rs_send.at[0, h, 0], rs_recv.at[0, h, 0], dn))
        first.append(remote(st1.at[h, 1], rc1.at[h, 1], rs_send.at[0, h, 1], rs_recv.at[0, h, 1], up))
        second.append(remote(st2.at[h, 0], rc2.at[h, 0], rs_send.at[1, h, 0], rs_recv.at[1, h, 0], dn))
        second.append(remote(st2.at[h, 1], rc2.at[h, 1], rs_send.at[1, h, 1], rs_recv.at[1, h, 1], up))
        up, dn = rings[1 - h]
        third.append(remote(st3.at[h, 0], rc3.at[h, 0], rs_send.at[2, h, 0], rs_recv.at[2, h, 0], dn))
        third.append(remote(st3.at[h, 1], rc3.at[h, 1], rs_send.at[2, h, 1], rs_recv.at[2, h, 1], up))
        fourth.append(remote(st4.at[h, 0], rc4.at[h, 0], rs_send.at[3, h, 0], rs_recv.at[3, h, 0], dn))
        fourth.append(remote(st4.at[h, 1], rc4.at[h, 1], rs_send.at[3, h, 1], rs_recv.at[3, h, 1], up))

    def reduce1(h):
        far = (spots[h] + 2) % 4
        st1[h, 0] = part_of(h, 0, far).astype(bf16)
        first[2 * h].start()
        st1[h, 1] = part_of(h, 1, far).astype(bf16)
        first[2 * h + 1].start()

    def reduce2(h):
        spot = spots[h]
        st2[h, 0, 1] = part_of(h, 1, (spot + 3) % 4).astype(bf16)
        st2[h, 1, 0] = part_of(h, 0, (spot + 1) % 4).astype(bf16)
        first[2 * h].wait_recv()
        st2[h, 0, 0] = (part_of(h, 0, (spot + 3) % 4) + rc1[h, 0].astype(f32)).astype(bf16)
        second[2 * h].start()
        first[2 * h + 1].wait_recv()
        st2[h, 1, 1] = (part_of(h, 1, (spot + 1) % 4) + rc1[h, 1].astype(f32)).astype(bf16)
        second[2 * h + 1].start()

    def reduce3(h):
        second[2 * h].wait_recv()
        second[2 * h + 1].wait_recv()
        for i in range(2):
            red[h, i] = part_of(h, i, spots[h]) + rc2[h, 0, i].astype(f32) + rc2[h, 1, i].astype(f32)
        spot = spots[1 - h]
        far = (spot + 2) % 4
        st3[h, 0] = red[h, 0, far]
        third[2 * h].start()
        st3[h, 1] = red[h, 1, far]
        third[2 * h + 1].start()
        st4[h, 0, 1] = red[h, 1, (spot + 3) % 4]
        st4[h, 1, 0] = red[h, 0, (spot + 1) % 4]

    def reduce4(h):
        spot = spots[1 - h]
        third[2 * h].wait_recv()
        st4[h, 0, 0] = red[h, 0, (spot + 3) % 4] + rc3[h, 0]
        fourth[2 * h].start()
        third[2 * h + 1].wait_recv()
        st4[h, 1, 1] = red[h, 1, (spot + 1) % 4] + rc3[h, 1]
        fourth[2 * h + 1].start()

    def x_copies(h):
        to_self = jnp.logical_and(x_hi == x_lo, h == x_lo)
        local = pltpu.make_async_copy(fin.at[h], rcx.at[x_hi], x_recv.at[x_hi])
        away = remote(fin.at[h], rcx.at[x_hi], x_send.at[h], x_recv.at[x_hi], x_from(h))
        return to_self, local, away

    def reduce5(h):
        fourth[2 * h].wait_recv()
        fourth[2 * h + 1].wait_recv()
        for i in range(2):
            fin[h, i] = red[h, i, spots[1 - h]] + rc4[h, 0, i] + rc4[h, 1, i]
        to_self, local, away = x_copies(h)

        @pl.when(to_self)
        def _():
            local.start()

        @pl.when(jnp.logical_not(to_self))
        def _():
            away.start()

    def finish(layer):
        for blk in range(2):
            s = 2 * blk + layer
            for n in range(4):
                t = (acc[:, lanes((s * 4 + n) * 256, 256)] * SCALE).T.astype(bf16)
                dq_s[s, :, lanes(n * 256, 128)] = t[:128]
                dq_s[s, :, lanes(n * 256 + 128, 128)] = t[128:]

    mine = pltpu.make_async_copy(dq_s.at[core], dq_out.at[:, own_cols], loc.at[2])
    back = [
        remote(dq_s.at[2 * flip + c_t], dq_out.at[:, own_cols], dq_send.at[n], dq_recv.at[n], mates[n])
        for n, (c_t, flip) in enumerate(((1 - core, 0), (core, 1), (1 - core, 1)))
    ]

    def rows(sweep, carry):
        layer = (core + 1 + sweep) % 2

        def cell(o, carry):
            for at, act in ((2, lambda: reduce1(1)), (6, lambda: reduce1(0)), (10, lambda: reduce2(1)), (12, lambda: reduce3(1))):
                @pl.when(jnp.logical_and(sweep == 1, o == at))
                def _(act=act):
                    act()

            kc = order(o)
            for blk in range(2):
                chunk(grads, blk, kc, [8 * blk + 4 * layer + n for n in range(4)])
            return carry

        lax.fori_loop(0, 16, cell, 0)
        finish(layer)

        @pl.when(sweep == 0)
        def _():
            back[0].start()
            back[2].start()

        return carry

    def order(o):
        pick = [
            8 + ((y + 2) % 4) * 2 + o,
            (o - 2) * 2 + 1 - z // 2,
            8 + ((y + 1 + 2 * ((o - 6) // 2) - (o - 6) // 4) % 4) * 2 + o % 2,
            (o - 12) * 2 + z // 2,
        ]
        g1, g2, g3 = (o + 14) // 16, (o + 10) // 16, (o + 4) // 16
        return pick[0] * (1 - g1) + pick[1] * (g1 - g2) + pick[2] * (g2 - g3) + pick[3] * g3

    lax.fori_loop(0, 2, rows, 0)
    back[1].start()
    mine.start()
    reduce2(0)
    reduce4(1)
    reduce3(0)
    reduce5(1)
    reduce4(0)
    reduce5(0)

    for s in range(2):
        pltpu.make_async_copy(fin.at[0], rcx.at[s], x_recv.at[s]).wait()
    dk_out[...] = ((rcx[0, 0] + rcx[1, 0]) * SCALE).astype(bf16)
    dv_out[...] = (rcx[0, 1] + rcx[1, 1]).astype(bf16)

    mine.wait()
    for copy in back:
        copy.wait()
    for copy in sum(ex[0] + ex[1] + ex[2], []) + near0 + onward0 + near1 + onward1 + first + second + third + fourth:
        copy.wait_send()
    for t in range(2):
        to_self, pairs = a_copies(t)
        for _, away in pairs:
            @pl.when(jnp.logical_not(to_self))
            def _(away=away):
                away.wait_send()

        to_self, _, away = x_copies(t)

        @pl.when(jnp.logical_not(to_self))
        def _(away=away):
            away.wait_send()


def body(queries, shared_keys, shared_values, out_grad):
    any_, vmem = pl.BlockSpec(memory_space=pl.ANY), pl.BlockSpec(memory_space=pltpu.VMEM)
    dma = pltpu.SemaphoreType.DMA
    big, small = (2, 2, 4, 128, 128), (2, 2, 2, 128, 128)
    dq, dk, dv = pl.pallas_call(
        kernel,
        out_shape=(
            jax.ShapeDtypeStruct((128, 4096), bf16),
            jax.ShapeDtypeStruct((128, 128), bf16),
            jax.ShapeDtypeStruct((128, 128), bf16),
        ),
        in_specs=[any_] * 4,
        out_specs=(any_, vmem, vmem),
        scratch_shapes=[
            pltpu.VMEM((4, 128, 1024), bf16),
            pltpu.VMEM((4, 128, 1024), bf16),
            pltpu.VMEM((4, 128, 1024), bf16),
            pltpu.VMEM((2, 2, 4, 4, 128, 128), bf16),
            pltpu.VMEM((128, 4096), bf16),
            pltpu.VMEM((128, 4096), bf16),
            pltpu.VMEM((128, 4096), bf16),
            pltpu.VMEM((128, 4096), f32),
            pltpu.VMEM((2, 2, 4, 4, 128, 128), f32),
            pltpu.VMEM((8, 4096), f32),
            pltpu.VMEM((8, 4096), f32),
            pltpu.VMEM((8, 4096), f32),
            pltpu.VMEM((1, 4096), f32),
            pltpu.VMEM((1, 4096), f32),
            pltpu.VMEM(big, bf16),
            pltpu.VMEM(big, bf16),
            pltpu.VMEM((2,) + big, bf16),
            pltpu.VMEM((2,) + big, bf16),
            pltpu.VMEM(big, f32),
            pltpu.VMEM((2, 2, 128, 128), f32),
            pltpu.VMEM((2, 2, 128, 128), f32),
            pltpu.VMEM(small, f32),
            pltpu.VMEM(small, f32),
            pltpu.VMEM((2, 2, 128, 128), f32),
            pltpu.VMEM((2, 2, 128, 128), f32),
            dma((2, 3, 2)), dma((2, 3, 2)), dma((3,)),
            dma((2, 2)), dma((2, 2)),
            dma((2, 2, 4)), dma((2, 2, 4)),
            dma((4, 2, 2)), dma((4, 2, 2)),
            dma((2,)), dma((2,)),
            dma((3,)), dma((3,)),
        ],
        compiler_params=pltpu.CompilerParams(
            collective_id=0, has_side_effects=True, vmem_limit_bytes=56 * 2**20
        ),
        cost_estimate=pl.CostEstimate(flops=16 * 10**9, bytes_accessed=4 * 2**20, transcendentals=18 * 10**6),
    )(queries[0], shared_keys, shared_values, out_grad[0])
    return dq[None], dk, dv


def solution(mesh):
    return jax.shard_map(
        body,
        mesh=mesh,
        in_specs=(P("pipe", "seq", None), P("seq", "pipe"), P("seq", "pipe"), P("pipe", "seq", None)),
        out_specs=(P("pipe", "seq", None), P("seq", "pipe"), P("seq", "pipe")),
        check_vma=False,
    )
```

```python
import functools
import math

import jax
import jax.numpy as jnp
from jax import lax
from jax.experimental import pallas as pl
from jax.experimental.pallas import tpu as pltpu
from jax.sharding import PartitionSpec as P

DH = 128
TOK = 128
CH = 256
SCALE = 1.0 / math.sqrt(DH)
EXPO = math.log2(math.e) / math.sqrt(DH)
f32, bf16 = jnp.float32, jnp.bfloat16
NN = (((1,), (0,)), ((), ()))


def dot(a, b):
    return lax.dot_general(a, b, NN, preferred_element_type=f32)


def lanes(start, size):
    return pl.ds(pl.multiple_of(start, 128), size)


def kernel(
    q_in, k_in, v_in, g_in,
    dq_out, dk_out, dv_out,
    q_s, g_s, dq_s, kv, q_t, g_t, k_t, acc, dkv,
    m8, l8, d8, top, rdot,
    st1, rc1, st2, rc2, red, st3, rc3, st4, rc4, fin, rcx,
    ex_send, ex_recv, loc, a_send, a_recv, clear_sem, y_send, y_recv, z_send, z_recv,
    rs_send, rs_recv, x_send, x_recv, dq_send, dq_recv,
):
    pipe = lax.axis_index("pipe")
    seq = lax.axis_index("seq")
    x_hi, core = pipe // 2, pipe % 2
    x_lo, y, z = seq // 16, (seq // 4) % 4, seq % 4
    head = 2 * x_lo + core

    def dev(x_hi_, core_, x_lo_, y_, z_):
        return {"pipe": x_hi_ * 2 + core_, "seq": x_lo_ * 16 + y_ * 4 + z_}

    def remote(src, dst, send, recv, to):
        return pltpu.make_async_remote_copy(
            src_ref=src, dst_ref=dst, send_sem=send, recv_sem=recv,
            device_id=to, device_id_type=pl.DeviceIdType.MESH,
        )

    mates = [
        dev(x_hi, 1 - core, x_lo, y, z),
        dev(x_hi, core, 1 - x_lo, 3 - y, z),
        dev(x_hi, 1 - core, 1 - x_lo, 3 - y, z),
    ]
    y_up, y_dn = dev(x_hi, core, x_lo, (y + 1) % 4, z), dev(x_hi, core, x_lo, (y + 3) % 4, z)
    z_up, z_dn = dev(x_hi, core, x_lo, y, (z + 1) % 4), dev(x_hi, core, x_lo, y, (z + 3) % 4)
    y_step = 1 - 2 * (y % 2)
    y_all = (dev(x_hi, core, x_lo, 3 - y, z), dev(x_hi, core, x_lo, y + y_step, z))
    gate = [mates[0], dev(x_hi, core, 1 - x_lo, y, z), dev(x_hi, 1 - core, 1 - x_lo, y, z)]
    z_all = (z_up, z_dn, dev(x_hi, core, x_lo, y, (z + 2) % 4))

    def x_to(t):
        return dev(t, core, x_hi, y, z)

    def x_from(s):
        return dev(x_lo, core, s, y, z)

    barrier = pltpu.get_barrier_semaphore()
    for peer in mates + list(y_all + z_all) + gate[1:]:
        pl.semaphore_signal(barrier, inc=1, device_id=peer, device_id_type=pl.DeviceIdType.MESH)
    for t in range(2):
        @pl.when(jnp.logical_not(jnp.logical_and(t == x_hi, x_lo == x_hi)))
        def _():
            pl.semaphore_signal(barrier, inc=1, device_id=x_to(t), device_id_type=pl.DeviceIdType.MESH)

        @pl.when(jnp.logical_not(jnp.logical_and(x_lo == x_hi, t == x_lo)))
        def _():
            pl.semaphore_signal(barrier, inc=1, device_id=x_from(t), device_id_type=pl.DeviceIdType.MESH)

    own_cols = lanes(head * 1024, 1024)
    own = [
        pltpu.make_async_copy(q_in.at[:, own_cols], q_s.at[core], loc.at[0]),
        pltpu.make_async_copy(g_in.at[:, own_cols], g_s.at[core], loc.at[1]),
    ]
    for copy in own:
        copy.start()

    def clear(i, carry):
        dkv[i // 8, (i // 4) % 2, i % 4] = jnp.zeros((4, 128, 128), f32)
        return carry

    lax.fori_loop(0, 16, clear, 0)
    acc[...] = jnp.zeros_like(acc)
    m8[...] = jnp.full_like(m8, -1e30)
    l8[...] = jnp.zeros_like(l8)
    d8[...] = jnp.zeros_like(d8)

    def tile2(ref, i):
        s, n = i // 4, i % 4
        return jnp.concatenate(
            [ref[s, :, lanes(n * 256, 128)], ref[s, :, lanes(n * 256 + 128, 128)]], axis=0
        )

    def prep(i, carry=0):
        cols = lanes(i * 256, 256)
        q_t[:, cols] = tile2(q_s, i).T
        g_t[:, cols] = tile2(g_s, i).T
        return carry

    for copy in own:
        copy.wait()
    lax.fori_loop(0, 4, lambda n, carry: prep(core * 4 + n), 0)

    @pl.when(x_hi == x_lo)
    def _():
        pl.semaphore_wait(barrier, 12)

    @pl.when(x_hi != x_lo)
    def _():
        pl.semaphore_wait(barrier, 14)

    def a_copies(t):
        to_self = jnp.logical_and(t == x_hi, x_lo == x_hi)
        pairs = []
        for i, src in enumerate((k_in, v_in)):
            dst = kv.at[i, x_lo, y, z]
            pairs.append((
                pltpu.make_async_copy(src, dst, a_recv.at[i, x_lo]),
                remote(src, dst, a_send.at[i, t], a_recv.at[i, x_lo], x_to(t)),
            ))
        return to_self, pairs

    for t in range(2):
        to_self, pairs = a_copies(t)
        for local, away in pairs:
            @pl.when(to_self)
            def _(local=local):
                local.start()

            @pl.when(jnp.logical_not(to_self))
            def _(away=away):
                away.start()

    def exchange(n, half):
        c_t, flip = ((1 - core, 0), (core, 1), (1 - core, 1))[n]
        x_t = (1 - x_lo) if flip else x_lo
        cols = lanes((2 * x_t + c_t) * 1024 + half * 512, 512)
        there = lanes(half * 512, 512)
        slot = 2 * flip + core
        return [
            remote(src.at[:, cols], dst.at[slot, :, there], ex_send.at[i, n, half], ex_recv.at[i, n, half], mates[n])
            for i, (src, dst) in enumerate(((q_in, q_s), (g_in, g_s)))
        ]

    ex = [[exchange(n, half) for half in range(2)] for n in range(3)]
    for half in range(2):
        for copy in ex[0][half]:
            copy.start()

    for i in range(2):
        for s in range(2):
            pltpu.make_async_copy(k_in, kv.at[i, s, y, z], a_recv.at[i, s]).wait()

    def y_of(g):
        base = y + (g // 2) * y_step
        return base + (g % 2) * (3 - 2 * base)

    def pair(g):
        return kv.at[:, :, y_of(g), z]

    y_copies = [
        remote(pair(g), pair(g), y_send.at[d], y_recv.at[d], y_all[to]) for d, (g, to) in enumerate(((0, 0), (0, 1), (1, 1)))
    ]
    z_sent = [
        [remote(pair(g), pair(g), z_send.at[g, d], z_recv.at[g, d], z_all[d]) for d in range(3)] for g in range(4)
    ]
    for copy in y_copies[:2] + z_sent[0]:
        copy.start()
    y_copies[0].wait()
    for peer in gate:
        pl.semaphore_signal(clear_sem, inc=1, device_id=peer, device_id_type=pl.DeviceIdType.MESH)
    for copy in [y_copies[2]] + z_sent[1]:
        copy.start()
    y_copies[1].wait_recv()
    for copy in z_sent[2]:
        copy.start()
    pl.semaphore_wait(clear_sem, 3)
    for half in range(2):
        for n in (1, 2):
            for copy in ex[n][half]:
                copy.start()
    y_copies[2].wait_recv()
    for copy in z_sent[3]:
        copy.start()
    for half in range(2):
        for copy in ex[0][half]:
            copy.wait_recv()
    lax.fori_loop(0, 4, lambda n, carry: prep((1 - core) * 4 + n), 0)

    def keys(i, kc):
        return kv[i, kc // 8, (kc // 2) % 4, pl.ds(2 * (kc % 2), 2)].reshape(CH, DH)

    def visible(pos, kc):
        key_pos = kc * CH + lax.broadcasted_iota(jnp.int32, (CH, 256), 0)
        query_pos = pos * TOK + (lax.broadcasted_iota(jnp.int32, (CH, 256), 1) & 127)
        return key_pos <= query_pos

    def stats(pos, kc, i, masked):
        cols = lanes(i * 256, 256)
        s = dot(keys(0, kc), q_t[:, cols])
        dp = dot(keys(1, kc), g_t[:, cols])
        if masked:
            s = jnp.where(visible(pos, kc), s, -1e30)
        s = s.reshape(CH // 8, 8, 256)
        dp = dp.reshape(CH // 8, 8, 256)
        old = m8[:, cols]
        new = jnp.maximum(old, jnp.max(s, axis=0))
        w = jnp.exp2((s - new) * EXPO)
        shrink = jnp.exp2((old - new) * EXPO)
        m8[:, cols] = new
        l8[:, cols] = l8[:, cols] * shrink + jnp.sum(w, axis=0)
        d8[:, cols] = d8[:, cols] * shrink + jnp.sum(w * dp, axis=0)

    def tile8(ref, s):
        return jnp.concatenate([ref[s, :, lanes(n * 128, 128)] for n in range(8)], axis=0)

    def grads(pos, kc, s, masked):
        at = (kc // 8, (kc // 2) % 4, pl.ds(2 * (kc % 2), 2))
        p_parts, ds_parts = [], []
        for n in range(4):
            cols = lanes(s * 1024 + n * 256, 256)
            scores = dot(keys(0, kc), q_t[:, cols])
            dp = dot(keys(1, kc), g_t[:, cols])
            p = jnp.exp2(scores * EXPO - top[:, cols])
            if masked:
                p = jnp.where(visible(pos, kc), p, 0.0)
            ds = p * (dp - rdot[:, cols])
            p_parts.append(p.astype(bf16))
            ds_parts.append(ds.astype(bf16))
        p_low, ds_low = jnp.concatenate(p_parts, axis=1), jnp.concatenate(ds_parts, axis=1)
        dkv[(1,) + at] += dot(p_low, tile8(g_s, s)).reshape(2, 128, 128)
        dkv[(0,) + at] += dot(ds_low, tile8(q_s, s)).reshape(2, 128, 128)
        acc[:, lanes(s * 1024, 1024)] += dot(k_t[:, lanes(kc * CH, CH)], ds_low)

    positions = (seq, 16 * (1 - x_lo) + 4 * (3 - y) + z)

    def chunk(fn, blk, kc, tiles):
        pos = positions[blk]

        @pl.when(kc < pos // 2)
        def _():
            for i in tiles:
                fn(pos, kc, i, False)

        @pl.when(kc == pos // 2)
        def _():
            for i in tiles:
                fn(pos, kc, i, True)

    def far_tiles(half):
        return [8 + 2 * half, 9 + 2 * half, 12 + 2 * half, 13 + 2 * half]

    def far_arrive(half):
        for n in (1, 2):
            for copy in ex[n][half]:
                copy.wait_recv()
        for i in far_tiles(half):
            prep(i)

    def first_rows(o, carry):
        g = o // 4

        @pl.when(o % 4 == 0)
        def _():
            for d in range(3):
                pltpu.make_async_copy(kv.at[:, :, 0, 0], kv.at[:, :, 0, 0], z_recv.at[g, d]).wait()

        @pl.when(o == 0)
        def _():
            far_arrive(0)

        kc = ((o // 2) % 2) * 8 + y_of(g) * 2 + o % 2
        k_t[:, lanes(kc * CH, CH)] = keys(0, kc).T
        chunk(stats, 0, kc, range(8))
        chunk(stats, 1, kc, far_tiles(0))
        return carry

    lax.fori_loop(0, 16, first_rows, 0)
    far_arrive(1)

    def last_rows(kc, carry):
        for i in far_tiles(1):
            stats(positions[1], kc, i, False)
        return carry

    lax.fori_loop(0, positions[1] // 2, last_rows, 0)
    for i in far_tiles(1):
        stats(positions[1], positions[1] // 2, i, True)

    high = jnp.max(m8[...], axis=0, keepdims=True)
    fold = jnp.exp2((m8[...] - high) * EXPO)
    total = jnp.sum(l8[...] * fold, axis=0, keepdims=True)
    top[...] = high * EXPO + jnp.log2(total)
    rdot[...] = jnp.sum(d8[...] * fold, axis=0, keepdims=True) / total

    def part_of(h, i, d):
        return dkv[i, 0, :, d] if h == 0 else dkv[i, 1, d, :]

    spots = (z, y)
    rings = ((z_up, z_dn), (y_up, y_dn))
    first, second, third, fourth = [], [], [], []
    for h in range(2):
        up, dn = rings[h]
        first.append(remote(st1.at[h, 0], rc1.at[h, 0], rs_send.at[0, h, 0], rs_recv.at[0, h, 0], dn))
        first.append(remote(st1.at[h, 1], rc1.at[h, 1], rs_send.at[0, h, 1], rs_recv.at[0, h, 1], up))
        second.append(remote(st2.at[h, 0], rc2.at[h, 0], rs_send.at[1, h, 0], rs_recv.at[1, h, 0], dn))
        second.append(remote(st2.at[h, 1], rc2.at[h, 1], rs_send.at[1, h, 1], rs_recv.at[1, h, 1], up))
        up, dn = rings[1 - h]
        third.append(remote(st3.at[h, 0], rc3.at[h, 0], rs_send.at[2, h, 0], rs_recv.at[2, h, 0], dn))
        third.append(remote(st3.at[h, 1], rc3.at[h, 1], rs_send.at[2, h, 1], rs_recv.at[2, h, 1], up))
        fourth.append(remote(st4.at[h, 0], rc4.at[h, 0], rs_send.at[3, h, 0], rs_recv.at[3, h, 0], dn))
        fourth.append(remote(st4.at[h, 1], rc4.at[h, 1], rs_send.at[3, h, 1], rs_recv.at[3, h, 1], up))

    def reduce1(h):
        far = (spots[h] + 2) % 4
        st1[h, 0] = part_of(h, 0, far).astype(bf16)
        first[2 * h].start()
        st1[h, 1] = part_of(h, 1, far).astype(bf16)
        first[2 * h + 1].start()

    def reduce2(h):
        spot = spots[h]
        st2[h, 0, 1] = part_of(h, 1, (spot + 3) % 4).astype(bf16)
        st2[h, 1, 0] = part_of(h, 0, (spot + 1) % 4).astype(bf16)
        first[2 * h].wait_recv()
        st2[h, 0, 0] = (part_of(h, 0, (spot + 3) % 4) + rc1[h, 0].astype(f32)).astype(bf16)
        second[2 * h].start()
        first[2 * h + 1].wait_recv()
        st2[h, 1, 1] = (part_of(h, 1, (spot + 1) % 4) + rc1[h, 1].astype(f32)).astype(bf16)
        second[2 * h + 1].start()

    def reduce3(h):
        second[2 * h].wait_recv()
        second[2 * h + 1].wait_recv()
        for i in range(2):
            red[h, i] = part_of(h, i, spots[h]) + rc2[h, 0, i].astype(f32) + rc2[h, 1, i].astype(f32)
        spot = spots[1 - h]
        far = (spot + 2) % 4
        st3[h, 0] = red[h, 0, far]
        third[2 * h].start()
        st3[h, 1] = red[h, 1, far]
        third[2 * h + 1].start()
        st4[h, 0, 1] = red[h, 1, (spot + 3) % 4]
        st4[h, 1, 0] = red[h, 0, (spot + 1) % 4]

    def reduce4(h):
        spot = spots[1 - h]
        third[2 * h].wait_recv()
        st4[h, 0, 0] = red[h, 0, (spot + 3) % 4] + rc3[h, 0]
        fourth[2 * h].start()
        third[2 * h + 1].wait_recv()
        st4[h, 1, 1] = red[h, 1, (spot + 1) % 4] + rc3[h, 1]
        fourth[2 * h + 1].start()

    def x_copies(h):
        to_self = jnp.logical_and(x_hi == x_lo, h == x_lo)
        local = pltpu.make_async_copy(fin.at[h], rcx.at[x_hi], x_recv.at[x_hi])
        away = remote(fin.at[h], rcx.at[x_hi], x_send.at[h], x_recv.at[x_hi], x_from(h))
        return to_self, local, away

    def reduce5(h):
        fourth[2 * h].wait_recv()
        fourth[2 * h + 1].wait_recv()
        for i in range(2):
            fin[h, i] = red[h, i, spots[1 - h]] + rc4[h, 0, i] + rc4[h, 1, i]
        to_self, local, away = x_copies(h)

        @pl.when(to_self)
        def _():
            local.start()

        @pl.when(jnp.logical_not(to_self))
        def _():
            away.start()

    def finish(layer):
        for blk in range(2):
            s = 2 * blk + layer
            for n in range(4):
                t = (acc[:, lanes((s * 4 + n) * 256, 256)] * SCALE).T.astype(bf16)
                dq_s[s, :, lanes(n * 256, 128)] = t[:128]
                dq_s[s, :, lanes(n * 256 + 128, 128)] = t[128:]

    mine = pltpu.make_async_copy(dq_s.at[core], dq_out.at[:, own_cols], loc.at[2])
    back = [
        remote(dq_s.at[2 * flip + c_t], dq_out.at[:, own_cols], dq_send.at[n], dq_recv.at[n], mates[n])
        for n, (c_t, flip) in enumerate(((1 - core, 0), (core, 1), (1 - core, 1)))
    ]

    def rows(sweep, carry):
        layer = (core + 1 + sweep) % 2

        def cell(o, carry):
            for at, act in ((2, lambda: reduce1(1)), (6, lambda: reduce1(0)), (10, lambda: reduce2(1))):
                @pl.when(jnp.logical_and(sweep == 1, o == at))
                def _(act=act):
                    act()

            kc = order(o)
            for blk in range(2):
                chunk(grads, blk, kc, [2 * blk + layer])
            return carry

        lax.fori_loop(0, 16, cell, 0)

        @pl.when(sweep == 1)
        def _():
            reduce2(0)

        finish(layer)

        @pl.when(sweep == 0)
        def _():
            back[0].start()
            back[2].start()

        return carry

    def order(o):
        pick = [
            8 + ((y + 2) % 4) * 2 + o,
            (o - 2) * 2 + 1 - z // 2,
            8 + ((y + 1 + 2 * ((o - 6) // 2) - (o - 6) // 4) % 4) * 2 + o % 2,
            (o - 12) * 2 + z // 2,
        ]
        g1, g2, g3 = (o + 14) // 16, (o + 10) // 16, (o + 4) // 16
        return pick[0] * (1 - g1) + pick[1] * (g1 - g2) + pick[2] * (g2 - g3) + pick[3] * g3

    lax.fori_loop(0, 2, rows, 0)
    back[1].start()
    mine.start()
    reduce3(1)
    reduce4(1)
    reduce3(0)
    reduce5(1)
    reduce4(0)
    reduce5(0)

    for s in range(2):
        pltpu.make_async_copy(fin.at[0], rcx.at[s], x_recv.at[s]).wait()
    dk_out[...] = ((rcx[0, 0] + rcx[1, 0]) * SCALE).astype(bf16)
    dv_out[...] = (rcx[0, 1] + rcx[1, 1]).astype(bf16)

    mine.wait()
    for copy in back:
        copy.wait()
    for copy in sum(ex[0] + ex[1] + ex[2], []) + y_copies[1:] + sum(z_sent, []) + first + second + third + fourth:
        copy.wait_send()
    for t in range(2):
        to_self, pairs = a_copies(t)
        for _, away in pairs:
            @pl.when(jnp.logical_not(to_self))
            def _(away=away):
                away.wait_send()

        to_self, _, away = x_copies(t)

        @pl.when(jnp.logical_not(to_self))
        def _(away=away):
            away.wait_send()


def body(queries, shared_keys, shared_values, out_grad):
    any_, vmem = pl.BlockSpec(memory_space=pl.ANY), pl.BlockSpec(memory_space=pltpu.VMEM)
    dma = pltpu.SemaphoreType.DMA
    big, small = (2, 2, 4, 128, 128), (2, 2, 2, 128, 128)
    dq, dk, dv = pl.pallas_call(
        kernel,
        out_shape=(
            jax.ShapeDtypeStruct((128, 4096), bf16),
            jax.ShapeDtypeStruct((128, 128), bf16),
            jax.ShapeDtypeStruct((128, 128), bf16),
        ),
        in_specs=[any_] * 4,
        out_specs=(any_, vmem, vmem),
        scratch_shapes=[
            pltpu.VMEM((4, 128, 1024), bf16),
            pltpu.VMEM((4, 128, 1024), bf16),
            pltpu.VMEM((4, 128, 1024), bf16),
            pltpu.VMEM((2, 2, 4, 4, 128, 128), bf16),
            pltpu.VMEM((128, 4096), bf16),
            pltpu.VMEM((128, 4096), bf16),
            pltpu.VMEM((128, 4096), bf16),
            pltpu.VMEM((128, 4096), f32),
            pltpu.VMEM((2, 2, 4, 4, 128, 128), f32),
            pltpu.VMEM((8, 4096), f32),
            pltpu.VMEM((8, 4096), f32),
            pltpu.VMEM((8, 4096), f32),
            pltpu.VMEM((1, 4096), f32),
            pltpu.VMEM((1, 4096), f32),
            pltpu.VMEM(big, bf16),
            pltpu.VMEM(big, bf16),
            pltpu.VMEM((2,) + big, bf16),
            pltpu.VMEM((2,) + big, bf16),
            pltpu.VMEM(big, f32),
            pltpu.VMEM((2, 2, 128, 128), f32),
            pltpu.VMEM((2, 2, 128, 128), f32),
            pltpu.VMEM(small, f32),
            pltpu.VMEM(small, f32),
            pltpu.VMEM((2, 2, 128, 128), f32),
            pltpu.VMEM((2, 2, 128, 128), f32),
            dma((2, 3, 2)), dma((2, 3, 2)), dma((3,)),
            dma((2, 2)), dma((2, 2)),
            pltpu.SemaphoreType.REGULAR,
            dma((3,)), dma((3,)), dma((4, 3)), dma((4, 3)),
            dma((4, 2, 2)), dma((4, 2, 2)),
            dma((2,)), dma((2,)),
            dma((3,)), dma((3,)),
        ],
        compiler_params=pltpu.CompilerParams(
            collective_id=0, has_side_effects=True, vmem_limit_bytes=56 * 2**20
        ),
        cost_estimate=pl.CostEstimate(flops=16 * 10**9, bytes_accessed=4 * 2**20, transcendentals=18 * 10**6),
    )(queries[0], shared_keys, shared_values, out_grad[0])
    return dq[None], dk, dv


def solution(mesh):
    return jax.shard_map(
        body,
        mesh=mesh,
        in_specs=(P("pipe", "seq", None), P("seq", "pipe"), P("seq", "pipe"), P("pipe", "seq", None)),
        out_specs=(P("pipe", "seq", None), P("seq", "pipe"), P("seq", "pipe")),
        check_vma=False,
    )
```

```python
import functools
import math

import jax
import jax.numpy as jnp
from jax import lax
from jax.experimental import pallas as pl
from jax.experimental.pallas import tpu as pltpu
from jax.sharding import PartitionSpec as P

DH = 128
TOK = 128
CH = 256
SCALE = 1.0 / math.sqrt(DH)
EXPO = math.log2(math.e) / math.sqrt(DH)
f32, bf16 = jnp.float32, jnp.bfloat16
NN = (((1,), (0,)), ((), ()))


def dot(a, b):
    return lax.dot_general(a, b, NN, preferred_element_type=f32)


def lanes(start, size):
    return pl.ds(pl.multiple_of(start, 128), size)


def kernel(
    q_in, k_in, v_in, g_in,
    dq_out, dk_out, dv_out,
    q_s, g_s, dq_s, kv, q_t, g_t, k_t, acc, dkv,
    m8, l8, d8, top, rdot,
    zst, zrc, fst, frc, cst, crc, fin, rcx,
    ex_send, ex_recv, loc, a_send, a_recv, clear_sem, y_send, y_recv, z_send, z_recv,
    zr_send, zr_recv, f_send, f_recv, c_send, c_recv, x_send, x_recv, dq_send, dq_recv,
):
    pipe = lax.axis_index("pipe")
    seq = lax.axis_index("seq")
    x_hi, core = pipe // 2, pipe % 2
    x_lo, y, z = seq // 16, (seq // 4) % 4, seq % 4
    head = 2 * x_lo + core

    def dev(x_hi_, core_, x_lo_, y_, z_):
        return {"pipe": x_hi_ * 2 + core_, "seq": x_lo_ * 16 + y_ * 4 + z_}

    def remote(src, dst, send, recv, to):
        return pltpu.make_async_remote_copy(
            src_ref=src, dst_ref=dst, send_sem=send, recv_sem=recv,
            device_id=to, device_id_type=pl.DeviceIdType.MESH,
        )

    mates = [
        dev(x_hi, 1 - core, x_lo, y, z),
        dev(x_hi, core, 1 - x_lo, 3 - y, z),
        dev(x_hi, 1 - core, 1 - x_lo, 3 - y, z),
    ]
    y_up, y_dn = dev(x_hi, core, x_lo, (y + 1) % 4, z), dev(x_hi, core, x_lo, (y + 3) % 4, z)
    z_up, z_dn = dev(x_hi, core, x_lo, y, (z + 1) % 4), dev(x_hi, core, x_lo, y, (z + 3) % 4)
    y_step = 1 - 2 * (y % 2)
    y_all = (dev(x_hi, core, x_lo, 3 - y, z), dev(x_hi, core, x_lo, y + y_step, z))
    gate = [mates[0], dev(x_hi, core, 1 - x_lo, y, z), dev(x_hi, 1 - core, 1 - x_lo, y, z)]
    z_all = (z_up, z_dn, dev(x_hi, core, x_lo, y, (z + 2) % 4))

    def x_to(t):
        return dev(t, core, x_hi, y, z)

    def x_from(s):
        return dev(x_lo, core, s, y, z)

    barrier = pltpu.get_barrier_semaphore()
    for peer in mates + list(y_all + z_all) + gate[1:]:
        pl.semaphore_signal(barrier, inc=1, device_id=peer, device_id_type=pl.DeviceIdType.MESH)
    for t in range(2):
        @pl.when(jnp.logical_not(jnp.logical_and(t == x_hi, x_lo == x_hi)))
        def _():
            pl.semaphore_signal(barrier, inc=1, device_id=x_to(t), device_id_type=pl.DeviceIdType.MESH)

        @pl.when(jnp.logical_not(jnp.logical_and(x_lo == x_hi, t == x_lo)))
        def _():
            pl.semaphore_signal(barrier, inc=1, device_id=x_from(t), device_id_type=pl.DeviceIdType.MESH)

    own_cols = lanes(head * 1024, 1024)
    own = [
        pltpu.make_async_copy(q_in.at[:, own_cols], q_s.at[core], loc.at[0]),
        pltpu.make_async_copy(g_in.at[:, own_cols], g_s.at[core], loc.at[1]),
    ]
    for copy in own:
        copy.start()

    def clear(i, carry):
        dkv[i // 8, (i // 4) % 2, i % 4] = jnp.zeros((4, 128, 128), f32)
        return carry

    lax.fori_loop(0, 16, clear, 0)
    acc[...] = jnp.zeros_like(acc)
    m8[...] = jnp.full_like(m8, -1e30)
    l8[...] = jnp.zeros_like(l8)
    d8[...] = jnp.zeros_like(d8)

    def tile2(ref, i):
        s, n = i // 4, i % 4
        return jnp.concatenate(
            [ref[s, :, lanes(n * 256, 128)], ref[s, :, lanes(n * 256 + 128, 128)]], axis=0
        )

    def prep(i, carry=0):
        cols = lanes(i * 256, 256)
        q_t[:, cols] = tile2(q_s, i).T
        g_t[:, cols] = tile2(g_s, i).T
        return carry

    for copy in own:
        copy.wait()
    lax.fori_loop(0, 4, lambda n, carry: prep(core * 4 + n), 0)

    @pl.when(x_hi == x_lo)
    def _():
        pl.semaphore_wait(barrier, 12)

    @pl.when(x_hi != x_lo)
    def _():
        pl.semaphore_wait(barrier, 14)

    def a_copies(t):
        to_self = jnp.logical_and(t == x_hi, x_lo == x_hi)
        pairs = []
        for i, src in enumerate((k_in, v_in)):
            dst = kv.at[i, x_lo, y, z]
            pairs.append((
                pltpu.make_async_copy(src, dst, a_recv.at[i, x_lo]),
                remote(src, dst, a_send.at[i, t], a_recv.at[i, x_lo], x_to(t)),
            ))
        return to_self, pairs

    for t in range(2):
        to_self, pairs = a_copies(t)
        for local, away in pairs:
            @pl.when(to_self)
            def _(local=local):
                local.start()

            @pl.when(jnp.logical_not(to_self))
            def _(away=away):
                away.start()

    def exchange(n, half):
        c_t, flip = ((1 - core, 0), (core, 1), (1 - core, 1))[n]
        x_t = (1 - x_lo) if flip else x_lo
        cols = lanes((2 * x_t + c_t) * 1024 + half * 512, 512)
        there = lanes(half * 512, 512)
        slot = 2 * flip + core
        return [
            remote(src.at[:, cols], dst.at[slot, :, there], ex_send.at[i, n, half], ex_recv.at[i, n, half], mates[n])
            for i, (src, dst) in enumerate(((q_in, q_s), (g_in, g_s)))
        ]

    ex = [[exchange(n, half) for half in range(2)] for n in range(3)]
    for half in range(2):
        for copy in ex[0][half]:
            copy.start()

    for i in range(2):
        for s in range(2):
            pltpu.make_async_copy(k_in, kv.at[i, s, y, z], a_recv.at[i, s]).wait()

    def y_of(g):
        base = y + (g // 2) * y_step
        return base + (g % 2) * (3 - 2 * base)

    def pair(g):
        return kv.at[:, :, y_of(g), z]

    y_copies = [
        remote(pair(g), pair(g), y_send.at[d], y_recv.at[d], y_all[to]) for d, (g, to) in enumerate(((0, 0), (0, 1), (1, 1)))
    ]
    z_sent = [
        [remote(pair(g), pair(g), z_send.at[g, d], z_recv.at[g, d], z_all[d]) for d in range(3)] for g in range(4)
    ]
    for copy in y_copies[:2] + z_sent[0]:
        copy.start()
    y_copies[0].wait()
    for peer in gate:
        pl.semaphore_signal(clear_sem, inc=1, device_id=peer, device_id_type=pl.DeviceIdType.MESH)
    for copy in [y_copies[2]] + z_sent[1]:
        copy.start()
    y_copies[1].wait_recv()
    for copy in z_sent[2]:
        copy.start()
    pl.semaphore_wait(clear_sem, 3)
    for half in range(2):
        for n in (1, 2):
            for copy in ex[n][half]:
                copy.start()
    y_copies[2].wait_recv()
    for copy in z_sent[3]:
        copy.start()
    for half in range(2):
        for copy in ex[0][half]:
            copy.wait_recv()
    lax.fori_loop(0, 4, lambda n, carry: prep((1 - core) * 4 + n), 0)

    def keys(i, kc):
        return kv[i, kc // 8, (kc // 2) % 4, pl.ds(2 * (kc % 2), 2)].reshape(CH, DH)

    def visible(pos, kc):
        key_pos = kc * CH + lax.broadcasted_iota(jnp.int32, (CH, 256), 0)
        query_pos = pos * TOK + (lax.broadcasted_iota(jnp.int32, (CH, 256), 1) & 127)
        return key_pos <= query_pos

    def stats(pos, kc, i, masked):
        cols = lanes(i * 256, 256)
        s = dot(keys(0, kc), q_t[:, cols])
        dp = dot(keys(1, kc), g_t[:, cols])
        if masked:
            s = jnp.where(visible(pos, kc), s, -1e30)
        s = s.reshape(CH // 8, 8, 256)
        dp = dp.reshape(CH // 8, 8, 256)
        old = m8[:, cols]
        new = jnp.maximum(old, jnp.max(s, axis=0))
        w = jnp.exp2((s - new) * EXPO)
        shrink = jnp.exp2((old - new) * EXPO)
        m8[:, cols] = new
        l8[:, cols] = l8[:, cols] * shrink + jnp.sum(w, axis=0)
        d8[:, cols] = d8[:, cols] * shrink + jnp.sum(w * dp, axis=0)

    def tile8(ref, s):
        return jnp.concatenate([ref[s, :, lanes(n * 128, 128)] for n in range(8)], axis=0)

    def grads(pos, kc, s, masked):
        at = (kc // 8, (kc // 2) % 4, pl.ds(2 * (kc % 2), 2))
        p_parts, ds_parts = [], []
        for n in range(4):
            cols = lanes(s * 1024 + n * 256, 256)
            scores = dot(keys(0, kc), q_t[:, cols])
            dp = dot(keys(1, kc), g_t[:, cols])
            p = jnp.exp2(scores * EXPO - top[:, cols])
            if masked:
                p = jnp.where(visible(pos, kc), p, 0.0)
            ds = p * (dp - rdot[:, cols])
            p_parts.append(p.astype(bf16))
            ds_parts.append(ds.astype(bf16))
        p_low, ds_low = jnp.concatenate(p_parts, axis=1), jnp.concatenate(ds_parts, axis=1)
        dkv[(1,) + at] += dot(p_low, tile8(g_s, s)).reshape(2, 128, 128)
        dkv[(0,) + at] += dot(ds_low, tile8(q_s, s)).reshape(2, 128, 128)
        acc[:, lanes(s * 1024, 1024)] += dot(k_t[:, lanes(kc * CH, CH)], ds_low)

    positions = (seq, 16 * (1 - x_lo) + 4 * (3 - y) + z)

    def chunk(fn, blk, kc, tiles):
        pos = positions[blk]

        @pl.when(kc < pos // 2)
        def _():
            for i in tiles:
                fn(pos, kc, i, False)

        @pl.when(kc == pos // 2)
        def _():
            for i in tiles:
                fn(pos, kc, i, True)

    def far_tiles(half):
        return [8 + 2 * half, 9 + 2 * half, 12 + 2 * half, 13 + 2 * half]

    def far_arrive(half):
        for n in (1, 2):
            for copy in ex[n][half]:
                copy.wait_recv()
        for i in far_tiles(half):
            prep(i)

    def first_rows(o, carry):
        g = o // 4

        @pl.when(o % 4 == 0)
        def _():
            for d in range(3):
                pltpu.make_async_copy(kv.at[:, :, 0, 0], kv.at[:, :, 0, 0], z_recv.at[g, d]).wait()

        @pl.when(o == 0)
        def _():
            far_arrive(0)

        kc = ((o // 2) % 2) * 8 + y_of(g) * 2 + o % 2
        k_t[:, lanes(kc * CH, CH)] = keys(0, kc).T
        chunk(stats, 0, kc, range(8))
        chunk(stats, 1, kc, far_tiles(0))
        return carry

    lax.fori_loop(0, 16, first_rows, 0)
    far_arrive(1)

    def last_rows(kc, carry):
        for i in far_tiles(1):
            stats(positions[1], kc, i, False)
        return carry

    lax.fori_loop(0, positions[1] // 2, last_rows, 0)
    for i in far_tiles(1):
        stats(positions[1], positions[1] // 2, i, True)

    high = jnp.max(m8[...], axis=0, keepdims=True)
    fold = jnp.exp2((m8[...] - high) * EXPO)
    total = jnp.sum(l8[...] * fold, axis=0, keepdims=True)
    top[...] = high * EXPO + jnp.log2(total)
    rdot[...] = jnp.sum(d8[...] * fold, axis=0, keepdims=True) / total

    def term(g, d):
        return dkv.at[:, :, y_of(g), (z + d) % 4]

    zr_copies = [
        [remote(zst.at[g, d], zrc.at[g, d], zr_send.at[g, d], zr_recv.at[g, d], z_all[d]) for d in range(3)] for g in range(4)
    ]
    f_copies = [remote(fst.at[n], frc.at[n], f_send.at[n], f_recv.at[n], y_all[1]) for n in range(2)]
    c_copy = remote(cst, crc, c_send, c_recv, y_all[0])

    def along_z(g):
        for d, step in enumerate((1, 3, 2)):
            zst[g, d] = term(g, step)[...].astype(bf16)
            zr_copies[g][d].start()

    def summed(g):
        for d in range(3):
            zr_copies[g][d].wait_recv()
        return term(g, 0)[...] + zrc[g, 0].astype(f32) + zrc[g, 1].astype(f32) + zrc[g, 2].astype(f32)

    def over_free(n):
        fst[n] = summed(3 - n).astype(bf16)
        f_copies[n].start()

    def over_cross():
        part = summed(1)
        f_copies[0].wait_recv()
        cst[...] = (part + frc[0].astype(f32)).astype(bf16)
        c_copy.start()

    def x_copies(h):
        to_self = jnp.logical_and(x_hi == x_lo, h == x_lo)
        local = pltpu.make_async_copy(fin.at[:, h], rcx.at[x_hi], x_recv.at[x_hi])
        away = remote(fin.at[:, h], rcx.at[x_hi], x_send.at[h], x_recv.at[x_hi], x_from(h))
        return to_self, local, away

    def along_x():
        part = summed(0)
        f_copies[1].wait_recv()
        c_copy.wait_recv()
        fin[...] = part + frc[1].astype(f32) + crc[...].astype(f32)
        for h in range(2):
            to_self, local, away = x_copies(h)

            @pl.when(to_self)
            def _(local=local):
                local.start()

            @pl.when(jnp.logical_not(to_self))
            def _(away=away):
                away.start()

    events = (
        (4, lambda: along_z(3)), (8, lambda: along_z(2)), (10, lambda: over_free(0)),
        (12, lambda: along_z(1)), (14, lambda: over_free(1)),
    )

    def second_rows(o, carry):
        for at, act in events:
            @pl.when(o == at)
            def _(act=act):
                act()

        kc = ((o // 2) % 2) * 8 + y_of(3 - o // 4) * 2 + o % 2
        for blk in range(2):
            chunk(grads, blk, kc, [2 * blk, 2 * blk + 1])
        return carry

    lax.fori_loop(0, 16, second_rows, 0)
    along_z(0)
    over_cross()

    def finish(s):
        for n in range(4):
            t = (acc[:, lanes((s * 4 + n) * 256, 256)] * SCALE).T.astype(bf16)
            dq_s[s, :, lanes(n * 256, 128)] = t[:128]
            dq_s[s, :, lanes(n * 256 + 128, 128)] = t[128:]

    back = [
        remote(dq_s.at[2 * flip + c_t], dq_out.at[:, own_cols], dq_send.at[n], dq_recv.at[n], mates[n])
        for n, (c_t, flip) in enumerate(((1 - core, 0), (core, 1), (1 - core, 1)))
    ]
    mine = pltpu.make_async_copy(dq_s.at[core], dq_out.at[:, own_cols], loc.at[2])
    finish(2 + core)
    back[1].start()
    finish(3 - core)
    back[2].start()
    finish(1 - core)
    back[0].start()
    finish(core)
    mine.start()
    along_x()

    for s in range(2):
        pltpu.make_async_copy(fin.at[:, 0], rcx.at[s], x_recv.at[s]).wait()
    dk_out[...] = ((rcx[0, 0] + rcx[1, 0]) * SCALE).astype(bf16)
    dv_out[...] = (rcx[0, 1] + rcx[1, 1]).astype(bf16)

    mine.wait()
    for copy in back:
        copy.wait()
    for copy in sum(ex[0] + ex[1] + ex[2], []) + y_copies[1:] + sum(z_sent, []) + sum(zr_copies, []) + f_copies + [c_copy]:
        copy.wait_send()
    for t in range(2):
        to_self, pairs = a_copies(t)
        for _, away in pairs:
            @pl.when(jnp.logical_not(to_self))
            def _(away=away):
                away.wait_send()

        to_self, _, away = x_copies(t)

        @pl.when(jnp.logical_not(to_self))
        def _(away=away):
            away.wait_send()


def body(queries, shared_keys, shared_values, out_grad):
    any_, vmem = pl.BlockSpec(memory_space=pl.ANY), pl.BlockSpec(memory_space=pltpu.VMEM)
    dma = pltpu.SemaphoreType.DMA
    part = (2, 2, 128, 128)
    dq, dk, dv = pl.pallas_call(
        kernel,
        out_shape=(
            jax.ShapeDtypeStruct((128, 4096), bf16),
            jax.ShapeDtypeStruct((128, 128), bf16),
            jax.ShapeDtypeStruct((128, 128), bf16),
        ),
        in_specs=[any_] * 4,
        out_specs=(any_, vmem, vmem),
        scratch_shapes=[
            pltpu.VMEM((4, 128, 1024), bf16),
            pltpu.VMEM((4, 128, 1024), bf16),
            pltpu.VMEM((4, 128, 1024), bf16),
            pltpu.VMEM((2, 2, 4, 4, 128, 128), bf16),
            pltpu.VMEM((128, 4096), bf16),
            pltpu.VMEM((128, 4096), bf16),
            pltpu.VMEM((128, 4096), bf16),
            pltpu.VMEM((128, 4096), f32),
            pltpu.VMEM((2, 2, 4, 4, 128, 128), f32),
            pltpu.VMEM((8, 4096), f32),
            pltpu.VMEM((8, 4096), f32),
            pltpu.VMEM((8, 4096), f32),
            pltpu.VMEM((1, 4096), f32),
            pltpu.VMEM((1, 4096), f32),
            pltpu.VMEM((4, 3) + part, bf16),
            pltpu.VMEM((4, 3) + part, bf16),
            pltpu.VMEM((2,) + part, bf16),
            pltpu.VMEM((2,) + part, bf16),
            pltpu.VMEM(part, bf16),
            pltpu.VMEM(part, bf16),
            pltpu.VMEM(part, f32),
            pltpu.VMEM(part, f32),
            dma((2, 3, 2)), dma((2, 3, 2)), dma((3,)),
            dma((2, 2)), dma((2, 2)),
            pltpu.SemaphoreType.REGULAR,
            dma((3,)), dma((3,)), dma((4, 3)), dma((4, 3)),
            dma((4, 3)), dma((4, 3)), dma((2,)), dma((2,)), dma, dma,
            dma((2,)), dma((2,)),
            dma((3,)), dma((3,)),
        ],
        compiler_params=pltpu.CompilerParams(
            collective_id=0, has_side_effects=True, vmem_limit_bytes=56 * 2**20
        ),
        cost_estimate=pl.CostEstimate(flops=16 * 10**9, bytes_accessed=4 * 2**20, transcendentals=18 * 10**6),
    )(queries[0], shared_keys, shared_values, out_grad[0])
    return dq[None], dk, dv


def solution(mesh):
    return jax.shard_map(
        body,
        mesh=mesh,
        in_specs=(P("pipe", "seq", None), P("seq", "pipe"), P("seq", "pipe"), P("pipe", "seq", None)),
        out_specs=(P("pipe", "seq", None), P("seq", "pipe"), P("seq", "pipe")),
        check_vma=False,
    )
```

```python
import functools
import math

import jax
import jax.numpy as jnp
from jax import lax
from jax.experimental import pallas as pl
from jax.experimental.pallas import tpu as pltpu
from jax.sharding import PartitionSpec as P

DH = 128
TOK = 128
CH = 256
SCALE = 1.0 / math.sqrt(DH)
EXPO = math.log2(math.e) / math.sqrt(DH)
f32, bf16 = jnp.float32, jnp.bfloat16
NN = (((1,), (0,)), ((), ()))


def dot(a, b):
    return lax.dot_general(a, b, NN, preferred_element_type=f32)


def lanes(start, size):
    return pl.ds(pl.multiple_of(start, 128), size)


def kernel(
    q_in, k_in, v_in, g_in,
    dq_out, dk_out, dv_out,
    q_s, g_s, dq_s, kv, q_t, g_t, k_t, acc, dkv,
    m8, l8, d8, top, rdot,
    zst, zrc, fst, frc, cst, crc, fin, rcx,
    ex_send, ex_recv, loc, a_send, a_recv, clear_sem, y_send, y_recv, z_send, z_recv,
    zr_send, zr_recv, zl_send, zl_recv, f_send, f_recv, c_send, c_recv, x_send, x_recv, dq_send, dq_recv,
):
    pipe = lax.axis_index("pipe")
    seq = lax.axis_index("seq")
    x_hi, core = pipe // 2, pipe % 2
    x_lo, y, z = seq // 16, (seq // 4) % 4, seq % 4
    head = 2 * x_lo + core

    def dev(x_hi_, core_, x_lo_, y_, z_):
        return {"pipe": x_hi_ * 2 + core_, "seq": x_lo_ * 16 + y_ * 4 + z_}

    def remote(src, dst, send, recv, to):
        return pltpu.make_async_remote_copy(
            src_ref=src, dst_ref=dst, send_sem=send, recv_sem=recv,
            device_id=to, device_id_type=pl.DeviceIdType.MESH,
        )

    mates = [
        dev(x_hi, 1 - core, x_lo, y, z),
        dev(x_hi, core, 1 - x_lo, 3 - y, z),
        dev(x_hi, 1 - core, 1 - x_lo, 3 - y, z),
    ]
    y_up, y_dn = dev(x_hi, core, x_lo, (y + 1) % 4, z), dev(x_hi, core, x_lo, (y + 3) % 4, z)
    z_up, z_dn = dev(x_hi, core, x_lo, y, (z + 1) % 4), dev(x_hi, core, x_lo, y, (z + 3) % 4)
    y_step = 1 - 2 * (y % 2)
    y_all = (dev(x_hi, core, x_lo, 3 - y, z), dev(x_hi, core, x_lo, y + y_step, z))
    gate = [mates[0], dev(x_hi, core, 1 - x_lo, y, z), dev(x_hi, 1 - core, 1 - x_lo, y, z)]
    z_all = (z_up, z_dn, dev(x_hi, core, x_lo, y, (z + 2) % 4))

    def x_to(t):
        return dev(t, core, x_hi, y, z)

    def x_from(s):
        return dev(x_lo, core, s, y, z)

    barrier = pltpu.get_barrier_semaphore()
    for peer in mates + list(y_all + z_all) + gate[1:]:
        pl.semaphore_signal(barrier, inc=1, device_id=peer, device_id_type=pl.DeviceIdType.MESH)
    for t in range(2):
        @pl.when(jnp.logical_not(jnp.logical_and(t == x_hi, x_lo == x_hi)))
        def _():
            pl.semaphore_signal(barrier, inc=1, device_id=x_to(t), device_id_type=pl.DeviceIdType.MESH)

        @pl.when(jnp.logical_not(jnp.logical_and(x_lo == x_hi, t == x_lo)))
        def _():
            pl.semaphore_signal(barrier, inc=1, device_id=x_from(t), device_id_type=pl.DeviceIdType.MESH)

    own_cols = lanes(head * 1024, 1024)
    own = [
        pltpu.make_async_copy(q_in.at[:, own_cols], q_s.at[core], loc.at[0]),
        pltpu.make_async_copy(g_in.at[:, own_cols], g_s.at[core], loc.at[1]),
    ]
    for copy in own:
        copy.start()

    def clear(i, carry):
        dkv[i // 8, (i // 4) % 2, i % 4] = jnp.zeros((4, 128, 128), f32)
        return carry

    lax.fori_loop(0, 16, clear, 0)
    acc[...] = jnp.zeros_like(acc)
    m8[...] = jnp.full_like(m8, -1e30)
    l8[...] = jnp.zeros_like(l8)
    d8[...] = jnp.zeros_like(d8)

    def tile2(ref, i):
        s, n = i // 4, i % 4
        return jnp.concatenate(
            [ref[s, :, lanes(n * 256, 128)], ref[s, :, lanes(n * 256 + 128, 128)]], axis=0
        )

    def prep(i, carry=0):
        cols = lanes(i * 256, 256)
        q_t[:, cols] = tile2(q_s, i).T
        g_t[:, cols] = tile2(g_s, i).T
        return carry

    for copy in own:
        copy.wait()
    lax.fori_loop(0, 4, lambda n, carry: prep(core * 4 + n), 0)

    @pl.when(x_hi == x_lo)
    def _():
        pl.semaphore_wait(barrier, 12)

    @pl.when(x_hi != x_lo)
    def _():
        pl.semaphore_wait(barrier, 14)

    def a_copies(t):
        to_self = jnp.logical_and(t == x_hi, x_lo == x_hi)
        pairs = []
        for i, src in enumerate((k_in, v_in)):
            dst = kv.at[i, x_lo, y, z]
            pairs.append((
                pltpu.make_async_copy(src, dst, a_recv.at[i, x_lo]),
                remote(src, dst, a_send.at[i, t], a_recv.at[i, x_lo], x_to(t)),
            ))
        return to_self, pairs

    for t in range(2):
        to_self, pairs = a_copies(t)
        for local, away in pairs:
            @pl.when(to_self)
            def _(local=local):
                local.start()

            @pl.when(jnp.logical_not(to_self))
            def _(away=away):
                away.start()

    def exchange(n, half):
        c_t, flip = ((1 - core, 0), (core, 1), (1 - core, 1))[n]
        x_t = (1 - x_lo) if flip else x_lo
        cols = lanes((2 * x_t + c_t) * 1024 + half * 512, 512)
        there = lanes(half * 512, 512)
        slot = 2 * flip + core
        return [
            remote(src.at[:, cols], dst.at[slot, :, there], ex_send.at[i, n, half], ex_recv.at[i, n, half], mates[n])
            for i, (src, dst) in enumerate(((q_in, q_s), (g_in, g_s)))
        ]

    ex = [[exchange(n, half) for half in range(2)] for n in range(3)]
    for half in range(2):
        for copy in ex[0][half]:
            copy.start()

    for i in range(2):
        for s in range(2):
            pltpu.make_async_copy(k_in, kv.at[i, s, y, z], a_recv.at[i, s]).wait()

    def y_of(g):
        base = y + (g // 2) * y_step
        return base + (g % 2) * (3 - 2 * base)

    def pair(g):
        return kv.at[:, :, y_of(g), z]

    y_copies = [
        remote(pair(g), pair(g), y_send.at[d], y_recv.at[d], y_all[to]) for d, (g, to) in enumerate(((0, 0), (0, 1), (1, 1)))
    ]
    z_sent = [
        [remote(pair(g), pair(g), z_send.at[g, d], z_recv.at[g, d], z_all[d]) for d in range(3)] for g in range(4)
    ]
    for copy in y_copies[:2] + z_sent[0]:
        copy.start()
    y_copies[0].wait()
    for peer in gate:
        pl.semaphore_signal(clear_sem, inc=1, device_id=peer, device_id_type=pl.DeviceIdType.MESH)
    for copy in [y_copies[2]] + z_sent[1]:
        copy.start()
    y_copies[1].wait_recv()
    for copy in z_sent[2]:
        copy.start()
    pl.semaphore_wait(clear_sem, 3)
    for half in range(2):
        for n in (1, 2):
            for copy in ex[n][half]:
                copy.start()
    y_copies[2].wait_recv()
    for copy in z_sent[3]:
        copy.start()
    for half in range(2):
        for copy in ex[0][half]:
            copy.wait_recv()
    lax.fori_loop(0, 4, lambda n, carry: prep((1 - core) * 4 + n), 0)

    def keys(i, kc):
        return kv[i, kc // 8, (kc // 2) % 4, pl.ds(2 * (kc % 2), 2)].reshape(CH, DH)

    def visible(pos, kc):
        key_pos = kc * CH + lax.broadcasted_iota(jnp.int32, (CH, 256), 0)
        query_pos = pos * TOK + (lax.broadcasted_iota(jnp.int32, (CH, 256), 1) & 127)
        return key_pos <= query_pos

    def stats(pos, kc, i, masked):
        cols = lanes(i * 256, 256)
        s = dot(keys(0, kc), q_t[:, cols])
        dp = dot(keys(1, kc), g_t[:, cols])
        if masked:
            s = jnp.where(visible(pos, kc), s, -1e30)
        s = s.reshape(CH // 8, 8, 256)
        dp = dp.reshape(CH // 8, 8, 256)
        old = m8[:, cols]
        new = jnp.maximum(old, jnp.max(s, axis=0))
        w = jnp.exp2((s - new) * EXPO)
        shrink = jnp.exp2((old - new) * EXPO)
        m8[:, cols] = new
        l8[:, cols] = l8[:, cols] * shrink + jnp.sum(w, axis=0)
        d8[:, cols] = d8[:, cols] * shrink + jnp.sum(w * dp, axis=0)

    def tile8(ref, s):
        return jnp.concatenate([ref[s, :, lanes(n * 128, 128)] for n in range(8)], axis=0)

    def grads(pos, kc, s, masked):
        at = (kc // 8, (kc // 2) % 4, pl.ds(2 * (kc % 2), 2))
        p_parts, ds_parts = [], []
        for n in range(4):
            cols = lanes(s * 1024 + n * 256, 256)
            scores = dot(keys(0, kc), q_t[:, cols])
            dp = dot(keys(1, kc), g_t[:, cols])
            p = jnp.exp2(scores * EXPO - top[:, cols])
            if masked:
                p = jnp.where(visible(pos, kc), p, 0.0)
            ds = p * (dp - rdot[:, cols])
            p_parts.append(p.astype(bf16))
            ds_parts.append(ds.astype(bf16))
        p_low, ds_low = jnp.concatenate(p_parts, axis=1), jnp.concatenate(ds_parts, axis=1)
        dkv[(1,) + at] += dot(p_low, tile8(g_s, s)).reshape(2, 128, 128)
        dkv[(0,) + at] += dot(ds_low, tile8(q_s, s)).reshape(2, 128, 128)
        acc[:, lanes(s * 1024, 1024)] += dot(k_t[:, lanes(kc * CH, CH)], ds_low)

    positions = (seq, 16 * (1 - x_lo) + 4 * (3 - y) + z)

    def chunk(fn, blk, kc, tiles):
        pos = positions[blk]

        @pl.when(kc < pos // 2)
        def _():
            for i in tiles:
                fn(pos, kc, i, False)

        @pl.when(kc == pos // 2)
        def _():
            for i in tiles:
                fn(pos, kc, i, True)

    def far_tiles(half):
        return [8 + 2 * half, 9 + 2 * half, 12 + 2 * half, 13 + 2 * half]

    def far_arrive(half):
        for n in (1, 2):
            for copy in ex[n][half]:
                copy.wait_recv()
        for i in far_tiles(half):
            prep(i)

    def first_rows(o, carry):
        g = o // 4

        @pl.when(o % 4 == 0)
        def _():
            for d in range(3):
                pltpu.make_async_copy(kv.at[:, :, 0, 0], kv.at[:, :, 0, 0], z_recv.at[g, d]).wait()

        @pl.when(o == 0)
        def _():
            far_arrive(0)

        kc = ((o // 2) % 2) * 8 + y_of(g) * 2 + o % 2
        k_t[:, lanes(kc * CH, CH)] = keys(0, kc).T
        chunk(stats, 0, kc, range(8))
        chunk(stats, 1, kc, far_tiles(0))
        return carry

    lax.fori_loop(0, 16, first_rows, 0)
    far_arrive(1)

    def last_rows(kc, carry):
        for i in far_tiles(1):
            stats(positions[1], kc, i, False)
        return carry

    lax.fori_loop(0, positions[1] // 2, last_rows, 0)
    for i in far_tiles(1):
        stats(positions[1], positions[1] // 2, i, True)

    high = jnp.max(m8[...], axis=0, keepdims=True)
    fold = jnp.exp2((m8[...] - high) * EXPO)
    total = jnp.sum(l8[...] * fold, axis=0, keepdims=True)
    top[...] = high * EXPO + jnp.log2(total)
    rdot[...] = jnp.sum(d8[...] * fold, axis=0, keepdims=True) / total

    z_spot = (z + 1 - 2 * (z % 2), (z + 2) % 4, 3 - z)
    z_peer = [dev(x_hi, core, x_lo, y, spot) for spot in z_spot]

    def term(g, spot):
        return dkv.at[:, :, y_of(g), spot]

    zr_copies = [
        [remote(zst.at[g, d], zrc.at[g, d], zr_send.at[g, d], zr_recv.at[g, d], z_peer[d]) for d in range(3)]
        for g in range(1, 4)
    ]
    last_copies = [
        [
            remote(zst.at[0, d, :, h], zrc.at[0, d, :, h], zl_send.at[h, d], zl_recv.at[h, d], z_peer[d])
            for d in range(3)
        ]
        for h in range(2)
    ]
    f_copies = [remote(fst.at[n], frc.at[n], f_send.at[n], f_recv.at[n], y_all[1]) for n in range(2)]
    c_copy = remote(cst, crc, c_send, c_recv, y_all[0])

    def along_z(g):
        for d in range(3):
            zst[g, d] = term(g, z_spot[d])[...].astype(bf16)
            zr_copies[g - 1][d].start()

    def last_along_z(h, parts):
        for d in parts:
            zst[0, d, :, h] = dkv[:, h, y, z_spot[d]].astype(bf16)
            last_copies[h][d].start()

    def summed(g):
        for copy in zr_copies[g - 1] if g else last_copies[0] + last_copies[1]:
            copy.wait_recv()
        return term(g, z)[...] + zrc[g, 0].astype(f32) + zrc[g, 1].astype(f32) + zrc[g, 2].astype(f32)

    def over_free(n):
        fst[n] = summed(3 - n).astype(bf16)
        f_copies[n].start()

    def over_cross():
        part = summed(1)
        f_copies[0].wait_recv()
        cst[...] = (part + frc[0].astype(f32)).astype(bf16)
        c_copy.start()

    def x_copies(h):
        to_self = jnp.logical_and(x_hi == x_lo, h == x_lo)
        local = pltpu.make_async_copy(fin.at[:, h], rcx.at[x_hi], x_recv.at[x_hi])
        away = remote(fin.at[:, h], rcx.at[x_hi], x_send.at[h], x_recv.at[x_hi], x_from(h))
        return to_self, local, away

    def along_x():
        part = summed(0)
        f_copies[1].wait_recv()
        c_copy.wait_recv()
        fin[...] = part + frc[1].astype(f32) + crc[...].astype(f32)
        for h in range(2):
            to_self, local, away = x_copies(h)

            @pl.when(to_self)
            def _(local=local):
                local.start()

            @pl.when(jnp.logical_not(to_self))
            def _(away=away):
                away.start()

    def finish(s):
        for n in range(4):
            t = (acc[:, lanes((s * 4 + n) * 256, 256)] * SCALE).T.astype(bf16)
            dq_s[s, :, lanes(n * 256, 128)] = t[:128]
            dq_s[s, :, lanes(n * 256 + 128, 128)] = t[128:]

    back = [
        remote(dq_s.at[2 * flip + c_t], dq_out.at[:, own_cols], dq_send.at[n], dq_recv.at[n], mates[n])
        for n, (c_t, flip) in enumerate(((1 - core, 0), (core, 1), (1 - core, 1)))
    ]
    mine = pltpu.make_async_copy(dq_s.at[core], dq_out.at[:, own_cols], loc.at[2])
    def when(cond, *acts):
        @pl.when(cond)
        def _():
            for act in acts:
                act()

    def chunk_at(g, o):
        return (o // 2) * 8 + y_of(g) * 2 + (z // 2 + 1 + o) % 2

    def second_rows(o, carry):
        when(o == 4, lambda: along_z(3))
        when(o == 8, lambda: along_z(2))
        when(o == 10, lambda: over_free(0))
        for blk in range(2):
            chunk(grads, blk, chunk_at(3 - o // 4, o % 4), [2 * blk, 2 * blk + 1])
        return carry

    lax.fori_loop(0, 12, second_rows, 0)
    along_z(1)

    def third_rows(o, carry):
        when(o == 2, lambda: over_free(1))
        when(
            o == 4,
            lambda: finish(3 - core), lambda: back[2].start(),
            lambda: finish(1 - core), lambda: back[0].start(),
        )
        layer = (core + 1 + o // 4) % 2
        for blk in range(2):
            chunk(grads, blk, chunk_at(0, o % 4), [2 * blk + layer])
        for h in range(2):
            when(o == 4 + 2 * h, lambda: last_along_z(h, (1, 2)))
            when(o == 5 + 2 * h, lambda: last_along_z(h, (0,)))
        return carry

    lax.fori_loop(0, 8, third_rows, 0)
    over_cross()
    finish(2 + core)
    back[1].start()
    finish(core)
    mine.start()
    along_x()

    for s in range(2):
        pltpu.make_async_copy(fin.at[:, 0], rcx.at[s], x_recv.at[s]).wait()
    dk_out[...] = ((rcx[0, 0] + rcx[1, 0]) * SCALE).astype(bf16)
    dv_out[...] = (rcx[0, 1] + rcx[1, 1]).astype(bf16)

    mine.wait()
    for copy in back:
        copy.wait()
    for copy in sum(ex[0] + ex[1] + ex[2], []) + y_copies[1:] + sum(z_sent, []) + sum(zr_copies + last_copies, []) + f_copies + [c_copy]:
        copy.wait_send()
    for t in range(2):
        to_self, pairs = a_copies(t)
        for _, away in pairs:
            @pl.when(jnp.logical_not(to_self))
            def _(away=away):
                away.wait_send()

        to_self, _, away = x_copies(t)

        @pl.when(jnp.logical_not(to_self))
        def _(away=away):
            away.wait_send()


def body(queries, shared_keys, shared_values, out_grad):
    any_, vmem = pl.BlockSpec(memory_space=pl.ANY), pl.BlockSpec(memory_space=pltpu.VMEM)
    dma = pltpu.SemaphoreType.DMA
    part = (2, 2, 128, 128)
    dq, dk, dv = pl.pallas_call(
        kernel,
        out_shape=(
            jax.ShapeDtypeStruct((128, 4096), bf16),
            jax.ShapeDtypeStruct((128, 128), bf16),
            jax.ShapeDtypeStruct((128, 128), bf16),
        ),
        in_specs=[any_] * 4,
        out_specs=(any_, vmem, vmem),
        scratch_shapes=[
            pltpu.VMEM((4, 128, 1024), bf16),
            pltpu.VMEM((4, 128, 1024), bf16),
            pltpu.VMEM((4, 128, 1024), bf16),
            pltpu.VMEM((2, 2, 4, 4, 128, 128), bf16),
            pltpu.VMEM((128, 4096), bf16),
            pltpu.VMEM((128, 4096), bf16),
            pltpu.VMEM((128, 4096), bf16),
            pltpu.VMEM((128, 4096), f32),
            pltpu.VMEM((2, 2, 4, 4, 128, 128), f32),
            pltpu.VMEM((8, 4096), f32),
            pltpu.VMEM((8, 4096), f32),
            pltpu.VMEM((8, 4096), f32),
            pltpu.VMEM((1, 4096), f32),
            pltpu.VMEM((1, 4096), f32),
            pltpu.VMEM((4, 3) + part, bf16),
            pltpu.VMEM((4, 3) + part, bf16),
            pltpu.VMEM((2,) + part, bf16),
            pltpu.VMEM((2,) + part, bf16),
            pltpu.VMEM(part, bf16),
            pltpu.VMEM(part, bf16),
            pltpu.VMEM(part, f32),
            pltpu.VMEM(part, f32),
            dma((2, 3, 2)), dma((2, 3, 2)), dma((3,)),
            dma((2, 2)), dma((2, 2)),
            pltpu.SemaphoreType.REGULAR,
            dma((3,)), dma((3,)), dma((4, 3)), dma((4, 3)),
            dma((4, 3)), dma((4, 3)), dma((2, 3)), dma((2, 3)), dma((2,)), dma((2,)), dma, dma,
            dma((2,)), dma((2,)),
            dma((3,)), dma((3,)),
        ],
        compiler_params=pltpu.CompilerParams(
            collective_id=0, has_side_effects=True, vmem_limit_bytes=56 * 2**20
        ),
        cost_estimate=pl.CostEstimate(flops=16 * 10**9, bytes_accessed=4 * 2**20, transcendentals=18 * 10**6),
    )(queries[0], shared_keys, shared_values, out_grad[0])
    return dq[None], dk, dv


def solution(mesh):
    return jax.shard_map(
        body,
        mesh=mesh,
        in_specs=(P("pipe", "seq", None), P("seq", "pipe"), P("seq", "pipe"), P("pipe", "seq", None)),
        out_specs=(P("pipe", "seq", None), P("seq", "pipe"), P("seq", "pipe")),
        check_vma=False,
    )
```

```python
import functools
import math

import jax
import jax.numpy as jnp
from jax import lax
from jax.experimental import pallas as pl
from jax.experimental.pallas import tpu as pltpu
from jax.sharding import PartitionSpec as P

DH = 128
TOK = 128
CH = 256
SCALE = 1.0 / math.sqrt(DH)
EXPO = math.log2(math.e) / math.sqrt(DH)
f32, bf16 = jnp.float32, jnp.bfloat16
NN = (((1,), (0,)), ((), ()))


def dot(a, b):
    return lax.dot_general(a, b, NN, preferred_element_type=f32)


def lanes(start, size):
    return pl.ds(pl.multiple_of(start, 128), size)


def kernel(
    q_in, k_in, v_in, g_in,
    dq_out, dk_out, dv_out,
    q_s, g_s, dq_s, kv, q_t, g_t, k_t, acc, dkv,
    m8, l8, d8, top, rdot,
    zst, zrc, fst, frc, cst, crc, fin, rcx,
    ex_send, ex_recv, loc, a_send, a_recv, clear_sem, y_send, y_recv, z_send, z_recv,
    zr_send, zr_recv, f_send, f_recv, c_send, c_recv, x_send, x_recv, dq_send, dq_recv,
):
    pipe = lax.axis_index("pipe")
    seq = lax.axis_index("seq")
    x_hi, core = pipe // 2, pipe % 2
    x_lo, y, z = seq // 16, (seq // 4) % 4, seq % 4
    head = 2 * x_lo + core

    def dev(x_hi_, core_, x_lo_, y_, z_):
        return {"pipe": x_hi_ * 2 + core_, "seq": x_lo_ * 16 + y_ * 4 + z_}

    def remote(src, dst, send, recv, to):
        return pltpu.make_async_remote_copy(
            src_ref=src, dst_ref=dst, send_sem=send, recv_sem=recv,
            device_id=to, device_id_type=pl.DeviceIdType.MESH,
        )

    mates = [
        dev(x_hi, 1 - core, x_lo, y, z),
        dev(x_hi, core, 1 - x_lo, 3 - y, z),
        dev(x_hi, 1 - core, 1 - x_lo, 3 - y, z),
    ]
    y_up, y_dn = dev(x_hi, core, x_lo, (y + 1) % 4, z), dev(x_hi, core, x_lo, (y + 3) % 4, z)
    z_up, z_dn = dev(x_hi, core, x_lo, y, (z + 1) % 4), dev(x_hi, core, x_lo, y, (z + 3) % 4)
    y_step = 1 - 2 * (y % 2)
    y_all = (dev(x_hi, core, x_lo, 3 - y, z), dev(x_hi, core, x_lo, y + y_step, z))
    gate = [mates[0], dev(x_hi, core, 1 - x_lo, y, z), dev(x_hi, 1 - core, 1 - x_lo, y, z)]
    z_all = (z_up, z_dn, dev(x_hi, core, x_lo, y, (z + 2) % 4))

    def x_to(t):
        return dev(t, core, x_hi, y, z)

    def x_from(s):
        return dev(x_lo, core, s, y, z)

    barrier = pltpu.get_barrier_semaphore()
    for peer in mates + list(y_all + z_all) + gate[1:]:
        pl.semaphore_signal(barrier, inc=1, device_id=peer, device_id_type=pl.DeviceIdType.MESH)
    for t in range(2):
        @pl.when(jnp.logical_not(jnp.logical_and(t == x_hi, x_lo == x_hi)))
        def _():
            pl.semaphore_signal(barrier, inc=1, device_id=x_to(t), device_id_type=pl.DeviceIdType.MESH)

        @pl.when(jnp.logical_not(jnp.logical_and(x_lo == x_hi, t == x_lo)))
        def _():
            pl.semaphore_signal(barrier, inc=1, device_id=x_from(t), device_id_type=pl.DeviceIdType.MESH)

    own_cols = lanes(head * 1024, 1024)
    own = [
        pltpu.make_async_copy(q_in.at[:, own_cols], q_s.at[core], loc.at[0]),
        pltpu.make_async_copy(g_in.at[:, own_cols], g_s.at[core], loc.at[1]),
    ]
    for copy in own:
        copy.start()

    def clear(i, carry):
        dkv[i // 8, (i // 4) % 2, i % 4] = jnp.zeros((4, 128, 128), f32)
        return carry

    lax.fori_loop(0, 16, clear, 0)
    acc[...] = jnp.zeros_like(acc)
    m8[...] = jnp.full_like(m8, -1e30)
    l8[...] = jnp.zeros_like(l8)
    d8[...] = jnp.zeros_like(d8)

    def tile2(ref, i):
        s, n = i // 4, i % 4
        return jnp.concatenate(
            [ref[s, :, lanes(n * 256, 128)], ref[s, :, lanes(n * 256 + 128, 128)]], axis=0
        )

    def prep(i, carry=0):
        cols = lanes(i * 256, 256)
        q_t[:, cols] = tile2(q_s, i).T
        g_t[:, cols] = tile2(g_s, i).T
        return carry

    for copy in own:
        copy.wait()
    lax.fori_loop(0, 4, lambda n, carry: prep(core * 4 + n), 0)

    @pl.when(x_hi == x_lo)
    def _():
        pl.semaphore_wait(barrier, 12)

    @pl.when(x_hi != x_lo)
    def _():
        pl.semaphore_wait(barrier, 14)

    def a_copies(t):
        to_self = jnp.logical_and(t == x_hi, x_lo == x_hi)
        pairs = []
        for i, src in enumerate((k_in, v_in)):
            dst = kv.at[i, x_lo, y, z]
            pairs.append((
                pltpu.make_async_copy(src, dst, a_recv.at[i, x_lo]),
                remote(src, dst, a_send.at[i, t], a_recv.at[i, x_lo], x_to(t)),
            ))
        return to_self, pairs

    for t in range(2):
        to_self, pairs = a_copies(t)
        for local, away in pairs:
            @pl.when(to_self)
            def _(local=local):
                local.start()

            @pl.when(jnp.logical_not(to_self))
            def _(away=away):
                away.start()

    def exchange(n, piece):
        start, width = ((0, 256), (256, 256), (512, 512))[piece]
        c_t, flip = ((1 - core, 0), (core, 1), (1 - core, 1))[n]
        x_t = (1 - x_lo) if flip else x_lo
        cols = lanes((2 * x_t + c_t) * 1024 + start, width)
        there = lanes(start, width)
        slot = 2 * flip + core
        return [
            remote(src.at[:, cols], dst.at[slot, :, there], ex_send.at[i, n, piece], ex_recv.at[i, n, piece], mates[n])
            for i, (src, dst) in enumerate(((q_in, q_s), (g_in, g_s)))
        ]

    ex = [[exchange(n, piece) for piece in range(3)] for n in range(3)]
    for n in (1, 2):
        for copy in ex[n][0]:
            copy.start()
    for piece in range(3):
        for copy in ex[0][piece]:
            copy.start()

    for i in range(2):
        for s in range(2):
            pltpu.make_async_copy(k_in, kv.at[i, s, y, z], a_recv.at[i, s]).wait()

    def y_of(g):
        base = y + (g // 2) * y_step
        return base + (g % 2) * (3 - 2 * base)

    def pair(g):
        return kv.at[:, :, y_of(g), z]

    y_copies = [
        remote(pair(g), pair(g), y_send.at[d], y_recv.at[d], y_all[to]) for d, (g, to) in enumerate(((0, 0), (0, 1), (1, 1)))
    ]
    z_sent = [
        [remote(pair(g), pair(g), z_send.at[g, d], z_recv.at[g, d], z_all[d]) for d in range(3)] for g in range(4)
    ]
    for copy in y_copies[:2] + z_sent[0]:
        copy.start()
    y_copies[0].wait()
    for peer in gate:
        pl.semaphore_signal(clear_sem, inc=1, device_id=peer, device_id_type=pl.DeviceIdType.MESH)
    for copy in [y_copies[2]] + z_sent[1]:
        copy.start()
    y_copies[1].wait_recv()
    for copy in z_sent[2]:
        copy.start()
    pl.semaphore_wait(clear_sem, 3)
    for piece in (1, 2):
        for n in (1, 2):
            for copy in ex[n][piece]:
                copy.start()
    y_copies[2].wait_recv()
    for copy in z_sent[3]:
        copy.start()
    for piece in range(3):
        for copy in ex[0][piece]:
            copy.wait_recv()
    lax.fori_loop(0, 4, lambda n, carry: prep((1 - core) * 4 + n), 0)

    def keys(i, kc):
        return kv[i, kc // 8, (kc // 2) % 4, pl.ds(2 * (kc % 2), 2)].reshape(CH, DH)

    def visible(pos, kc):
        key_pos = kc * CH + lax.broadcasted_iota(jnp.int32, (CH, 256), 0)
        query_pos = pos * TOK + (lax.broadcasted_iota(jnp.int32, (CH, 256), 1) & 127)
        return key_pos <= query_pos

    def stats(pos, kc, i, masked):
        cols = lanes(i * 256, 256)
        s = dot(keys(0, kc), q_t[:, cols])
        dp = dot(keys(1, kc), g_t[:, cols])
        if masked:
            s = jnp.where(visible(pos, kc), s, -1e30)
        s = s.reshape(CH // 8, 8, 256)
        dp = dp.reshape(CH // 8, 8, 256)
        old = m8[:, cols]
        new = jnp.maximum(old, jnp.max(s, axis=0))
        w = jnp.exp2((s - new) * EXPO)
        shrink = jnp.exp2((old - new) * EXPO)
        m8[:, cols] = new
        l8[:, cols] = l8[:, cols] * shrink + jnp.sum(w, axis=0)
        d8[:, cols] = d8[:, cols] * shrink + jnp.sum(w * dp, axis=0)

    def tile8(ref, s):
        return jnp.concatenate([ref[s, :, lanes(n * 128, 128)] for n in range(8)], axis=0)

    def grads(pos, kc, s, masked):
        at = (kc // 8, (kc // 2) % 4, pl.ds(2 * (kc % 2), 2))
        p_parts, ds_parts = [], []
        for n in range(4):
            cols = lanes(s * 1024 + n * 256, 256)
            scores = dot(keys(0, kc), q_t[:, cols])
            dp = dot(keys(1, kc), g_t[:, cols])
            p = jnp.exp2(scores * EXPO - top[:, cols])
            if masked:
                p = jnp.where(visible(pos, kc), p, 0.0)
            ds = p * (dp - rdot[:, cols])
            p_parts.append(p.astype(bf16))
            ds_parts.append(ds.astype(bf16))
        p_low, ds_low = jnp.concatenate(p_parts, axis=1), jnp.concatenate(ds_parts, axis=1)
        dkv[(1,) + at] += dot(p_low, tile8(g_s, s)).reshape(2, 128, 128)
        dkv[(0,) + at] += dot(ds_low, tile8(q_s, s)).reshape(2, 128, 128)
        acc[:, lanes(s * 1024, 1024)] += dot(k_t[:, lanes(kc * CH, CH)], ds_low)

    positions = (seq, 16 * (1 - x_lo) + 4 * (3 - y) + z)

    def chunk(fn, blk, kc, tiles):
        pos = positions[blk]

        @pl.when(kc < pos // 2)
        def _():
            for i in tiles:
                fn(pos, kc, i, False)

        @pl.when(kc == pos // 2)
        def _():
            for i in tiles:
                fn(pos, kc, i, True)

    def far_tiles(half):
        return [8 + 2 * half, 9 + 2 * half, 12 + 2 * half, 13 + 2 * half]

    def far_arrive(half):
        for n in (1, 2):
            for copy in ex[n][2] if half else ex[n][0] + ex[n][1]:
                copy.wait_recv()
        for i in far_tiles(half):
            prep(i)

    def first_rows(o, carry):
        g = o // 4

        @pl.when(o % 4 == 0)
        def _():
            for d in range(3):
                pltpu.make_async_copy(kv.at[:, :, 0, 0], kv.at[:, :, 0, 0], z_recv.at[g, d]).wait()

        @pl.when(o == 0)
        def _():
            far_arrive(0)

        kc = ((o // 2) % 2) * 8 + y_of(g) * 2 + o % 2
        k_t[:, lanes(kc * CH, CH)] = keys(0, kc).T
        chunk(stats, 0, kc, range(8))
        chunk(stats, 1, kc, far_tiles(0))
        return carry

    lax.fori_loop(0, 16, first_rows, 0)
    far_arrive(1)

    def last_rows(kc, carry):
        for i in far_tiles(1):
            stats(positions[1], kc, i, False)
        return carry

    lax.fori_loop(0, positions[1] // 2, last_rows, 0)
    for i in far_tiles(1):
        stats(positions[1], positions[1] // 2, i, True)

    high = jnp.max(m8[...], axis=0, keepdims=True)
    fold = jnp.exp2((m8[...] - high) * EXPO)
    total = jnp.sum(l8[...] * fold, axis=0, keepdims=True)
    top[...] = high * EXPO + jnp.log2(total)
    rdot[...] = jnp.sum(d8[...] * fold, axis=0, keepdims=True) / total

    z_spot = (z + 1 - 2 * (z % 2), (z + 2) % 4, 3 - z)
    z_peer = [dev(x_hi, core, x_lo, y, spot) for spot in z_spot]

    def term(g, spot):
        return dkv.at[:, :, y_of(g), spot]

    def z_copy(g, h, d):
        return remote(zst.at[g, d, :, h], zrc.at[g, d, :, h], zr_send.at[g, h, d], zr_recv.at[g, h, d], z_peer[d])

    zr_copies = [[z_copy(g, h, d) for h in range(2) for d in range(3)] for g in range(4)]
    f_copies = [remote(fst.at[n], frc.at[n], f_send.at[n], f_recv.at[n], y_all[1]) for n in range(2)]
    c_copy = remote(cst, crc, c_send, c_recv, y_all[0])

    def along_z(g, h, parts):
        for d in parts:
            zst[g, d, :, h] = dkv[:, h, y_of(g), z_spot[d]].astype(bf16)
            z_copy(g, h, d).start()

    def summed(g):
        for copy in zr_copies[g]:
            copy.wait_recv()
        return term(g, z)[...] + zrc[g, 0].astype(f32) + zrc[g, 1].astype(f32) + zrc[g, 2].astype(f32)

    def over_free(n):
        fst[n] = summed(3 - n).astype(bf16)
        f_copies[n].start()

    def over_cross():
        part = summed(1)
        f_copies[0].wait_recv()
        cst[...] = (part + frc[0].astype(f32)).astype(bf16)
        c_copy.start()

    def x_copies(h):
        to_self = jnp.logical_and(x_hi == x_lo, h == x_lo)
        local = pltpu.make_async_copy(fin.at[:, h], rcx.at[x_hi], x_recv.at[x_hi])
        away = remote(fin.at[:, h], rcx.at[x_hi], x_send.at[h], x_recv.at[x_hi], x_from(h))
        return to_self, local, away

    def along_x():
        part = summed(0)
        f_copies[1].wait_recv()
        c_copy.wait_recv()
        fin[...] = (part + frc[1].astype(f32) + crc[...].astype(f32)).astype(bf16)
        for h in range(2):
            to_self, local, away = x_copies(h)

            @pl.when(to_self)
            def _(local=local):
                local.start()

            @pl.when(jnp.logical_not(to_self))
            def _(away=away):
                away.start()

    def finish(s):
        for n in range(4):
            t = (acc[:, lanes((s * 4 + n) * 256, 256)] * SCALE).T.astype(bf16)
            dq_s[s, :, lanes(n * 256, 128)] = t[:128]
            dq_s[s, :, lanes(n * 256 + 128, 128)] = t[128:]

    back = [
        remote(dq_s.at[2 * flip + c_t], dq_out.at[:, own_cols], dq_send.at[n], dq_recv.at[n], mates[n])
        for n, (c_t, flip) in enumerate(((1 - core, 0), (core, 1), (1 - core, 1)))
    ]
    mine = pltpu.make_async_copy(dq_s.at[core], dq_out.at[:, own_cols], loc.at[2])
    def when(cond, *acts):
        @pl.when(cond)
        def _():
            for act in acts:
                act()

    def chunk_at(g, o):
        return (o // 2) * 8 + y_of(g) * 2 + (z // 2 + 1 + o) % 2

    def send_parts(g, o):
        for h in range(2):
            when(o == 2 * h, lambda: along_z(g, h, (1, 2)))
            when(o == 2 * h + 1, lambda: along_z(g, h, (0,)))

    def second_rows(o, carry):
        when(o == 8, lambda: over_free(0))
        for blk in range(2):
            chunk(grads, blk, chunk_at(3 - o // 4, o % 4), [2 * blk, 2 * blk + 1])
        send_parts(3 - o // 4, o % 4)
        return carry

    lax.fori_loop(0, 12, second_rows, 0)

    def third_rows(o, carry):
        when(o == 0, lambda: over_free(1))
        when(
            o == 4, over_cross,
            lambda: finish(3 - core), lambda: back[2].start(),
            lambda: finish(1 - core), lambda: back[0].start(),
        )
        layer = (core + 1 + o // 4) % 2
        for blk in range(2):
            chunk(grads, blk, chunk_at(0, o % 4), [2 * blk + layer])
        send_parts(0, o - 4)
        return carry

    lax.fori_loop(0, 8, third_rows, 0)
    finish(2 + core)
    back[1].start()
    finish(core)
    mine.start()
    along_x()

    for s in range(2):
        pltpu.make_async_copy(fin.at[:, 0], rcx.at[s], x_recv.at[s]).wait()
    total = rcx[0].astype(f32) + rcx[1].astype(f32)
    dk_out[...] = (total[0] * SCALE).astype(bf16)
    dv_out[...] = total[1].astype(bf16)

    mine.wait()
    for copy in back:
        copy.wait()
    for copy in sum(ex[0] + ex[1] + ex[2], []) + y_copies[1:] + sum(z_sent, []) + sum(zr_copies, []) + f_copies + [c_copy]:
        copy.wait_send()
    for t in range(2):
        to_self, pairs = a_copies(t)
        for _, away in pairs:
            @pl.when(jnp.logical_not(to_self))
            def _(away=away):
                away.wait_send()

        to_self, _, away = x_copies(t)

        @pl.when(jnp.logical_not(to_self))
        def _(away=away):
            away.wait_send()


def body(queries, shared_keys, shared_values, out_grad):
    any_, vmem = pl.BlockSpec(memory_space=pl.ANY), pl.BlockSpec(memory_space=pltpu.VMEM)
    dma = pltpu.SemaphoreType.DMA
    part = (2, 2, 128, 128)
    dq, dk, dv = pl.pallas_call(
        kernel,
        out_shape=(
            jax.ShapeDtypeStruct((128, 4096), bf16),
            jax.ShapeDtypeStruct((128, 128), bf16),
            jax.ShapeDtypeStruct((128, 128), bf16),
        ),
        in_specs=[any_] * 4,
        out_specs=(any_, vmem, vmem),
        scratch_shapes=[
            pltpu.VMEM((4, 128, 1024), bf16),
            pltpu.VMEM((4, 128, 1024), bf16),
            pltpu.VMEM((4, 128, 1024), bf16),
            pltpu.VMEM((2, 2, 4, 4, 128, 128), bf16),
            pltpu.VMEM((128, 4096), bf16),
            pltpu.VMEM((128, 4096), bf16),
            pltpu.VMEM((128, 4096), bf16),
            pltpu.VMEM((128, 4096), f32),
            pltpu.VMEM((2, 2, 4, 4, 128, 128), f32),
            pltpu.VMEM((8, 4096), f32),
            pltpu.VMEM((8, 4096), f32),
            pltpu.VMEM((8, 4096), f32),
            pltpu.VMEM((1, 4096), f32),
            pltpu.VMEM((1, 4096), f32),
            pltpu.VMEM((4, 3) + part, bf16),
            pltpu.VMEM((4, 3) + part, bf16),
            pltpu.VMEM((2,) + part, bf16),
            pltpu.VMEM((2,) + part, bf16),
            pltpu.VMEM(part, bf16),
            pltpu.VMEM(part, bf16),
            pltpu.VMEM(part, bf16),
            pltpu.VMEM(part, bf16),
            dma((2, 3, 3)), dma((2, 3, 3)), dma((3,)),
            dma((2, 2)), dma((2, 2)),
            pltpu.SemaphoreType.REGULAR,
            dma((3,)), dma((3,)), dma((4, 3)), dma((4, 3)),
            dma((4, 2, 3)), dma((4, 2, 3)), dma((2,)), dma((2,)), dma, dma,
            dma((2,)), dma((2,)),
            dma((3,)), dma((3,)),
        ],
        compiler_params=pltpu.CompilerParams(
            collective_id=0, has_side_effects=True, vmem_limit_bytes=56 * 2**20
        ),
        cost_estimate=pl.CostEstimate(flops=16 * 10**9, bytes_accessed=4 * 2**20, transcendentals=18 * 10**6),
    )(queries[0], shared_keys, shared_values, out_grad[0])
    return dq[None], dk, dv


def solution(mesh):
    return jax.shard_map(
        body,
        mesh=mesh,
        in_specs=(P("pipe", "seq", None), P("seq", "pipe"), P("seq", "pipe"), P("pipe", "seq", None)),
        out_specs=(P("pipe", "seq", None), P("seq", "pipe"), P("seq", "pipe")),
        check_vma=False,
    )
```

```python
import functools
import math

import jax
import jax.numpy as jnp
from jax import lax
from jax.experimental import pallas as pl
from jax.experimental.pallas import tpu as pltpu
from jax.sharding import PartitionSpec as P

DH = 128
TOK = 128
CH = 256
SCALE = 1.0 / math.sqrt(DH)
EXPO = math.log2(math.e) / math.sqrt(DH)
f32, bf16 = jnp.float32, jnp.bfloat16
NN = (((1,), (0,)), ((), ()))


def dot(a, b):
    return lax.dot_general(a, b, NN, preferred_element_type=f32)


def lanes(start, size):
    return pl.ds(pl.multiple_of(start, 128), size)


def kernel(
    q_in, k_in, v_in, g_in,
    dq_out, dk_out, dv_out,
    q_s, g_s, dq_s, kv, q_t, g_t, k_t, acc, dkv,
    m8, l8, d8, top, rdot,
    zst, zrc, fst, frc, cst, crc, fin, rcx,
    ex_send, ex_recv, loc, a_send, a_recv, clear_sem, y_send, y_recv, z_send, z_recv,
    zr_send, zr_recv, f_send, f_recv, c_send, c_recv, x_send, x_recv, dq_send, dq_recv,
):
    pipe = lax.axis_index("pipe")
    seq = lax.axis_index("seq")
    x_hi, core = pipe // 2, pipe % 2
    x_lo, y, z = seq // 16, (seq // 4) % 4, seq % 4
    head = 2 * x_lo + core

    def dev(x_hi_, core_, x_lo_, y_, z_):
        return {"pipe": x_hi_ * 2 + core_, "seq": x_lo_ * 16 + y_ * 4 + z_}

    def remote(src, dst, send, recv, to):
        return pltpu.make_async_remote_copy(
            src_ref=src, dst_ref=dst, send_sem=send, recv_sem=recv,
            device_id=to, device_id_type=pl.DeviceIdType.MESH,
        )

    mates = [
        dev(x_hi, 1 - core, x_lo, y, z),
        dev(x_hi, core, 1 - x_lo, 3 - y, z),
        dev(x_hi, 1 - core, 1 - x_lo, 3 - y, z),
    ]
    y_up, y_dn = dev(x_hi, core, x_lo, (y + 1) % 4, z), dev(x_hi, core, x_lo, (y + 3) % 4, z)
    z_up, z_dn = dev(x_hi, core, x_lo, y, (z + 1) % 4), dev(x_hi, core, x_lo, y, (z + 3) % 4)
    y_step = 1 - 2 * (y % 2)
    y_all = (dev(x_hi, core, x_lo, 3 - y, z), dev(x_hi, core, x_lo, y + y_step, z))
    gate = [mates[0], dev(x_hi, core, 1 - x_lo, y, z), dev(x_hi, 1 - core, 1 - x_lo, y, z)]
    z_all = (z_up, z_dn, dev(x_hi, core, x_lo, y, (z + 2) % 4))

    def x_to(t):
        return dev(t, core, x_hi, y, z)

    def x_from(s):
        return dev(x_lo, core, s, y, z)

    barrier = pltpu.get_barrier_semaphore()
    for peer in mates + list(y_all + z_all) + gate[1:]:
        pl.semaphore_signal(barrier, inc=1, device_id=peer, device_id_type=pl.DeviceIdType.MESH)
    for t in range(2):
        @pl.when(jnp.logical_not(jnp.logical_and(t == x_hi, x_lo == x_hi)))
        def _():
            pl.semaphore_signal(barrier, inc=1, device_id=x_to(t), device_id_type=pl.DeviceIdType.MESH)

        @pl.when(jnp.logical_not(jnp.logical_and(x_lo == x_hi, t == x_lo)))
        def _():
            pl.semaphore_signal(barrier, inc=1, device_id=x_from(t), device_id_type=pl.DeviceIdType.MESH)

    own_cols = lanes(head * 1024, 1024)
    own = [
        pltpu.make_async_copy(q_in.at[:, own_cols], q_s.at[core], loc.at[0]),
        pltpu.make_async_copy(g_in.at[:, own_cols], g_s.at[core], loc.at[1]),
    ]
    for copy in own:
        copy.start()

    def clear(i, carry):
        dkv[i // 8, (i // 4) % 2, i % 4] = jnp.zeros((4, 128, 128), f32)
        return carry

    lax.fori_loop(0, 16, clear, 0)
    acc[...] = jnp.zeros_like(acc)
    m8[...] = jnp.full_like(m8, -1e30)
    l8[...] = jnp.zeros_like(l8)
    d8[...] = jnp.zeros_like(d8)

    def tile2(ref, i):
        s, n = i // 4, i % 4
        return jnp.concatenate(
            [ref[s, :, lanes(n * 256, 128)], ref[s, :, lanes(n * 256 + 128, 128)]], axis=0
        )

    def prep(i, carry=0):
        cols = lanes(i * 256, 256)
        q_t[:, cols] = tile2(q_s, i).T
        g_t[:, cols] = tile2(g_s, i).T
        return carry

    for copy in own:
        copy.wait()
    lax.fori_loop(0, 4, lambda n, carry: prep(core * 4 + n), 0)

    @pl.when(x_hi == x_lo)
    def _():
        pl.semaphore_wait(barrier, 12)

    @pl.when(x_hi != x_lo)
    def _():
        pl.semaphore_wait(barrier, 14)

    def a_copies(t):
        to_self = jnp.logical_and(t == x_hi, x_lo == x_hi)
        pairs = []
        for i, src in enumerate((k_in, v_in)):
            dst = kv.at[i, x_lo, y, z]
            pairs.append((
                pltpu.make_async_copy(src, dst, a_recv.at[i, x_lo]),
                remote(src, dst, a_send.at[i, t], a_recv.at[i, x_lo], x_to(t)),
            ))
        return to_self, pairs

    for t in range(2):
        to_self, pairs = a_copies(t)
        for local, away in pairs:
            @pl.when(to_self)
            def _(local=local):
                local.start()

            @pl.when(jnp.logical_not(to_self))
            def _(away=away):
                away.start()

    def exchange(n, piece):
        start, width = ((0, 256), (256, 256), (512, 512))[piece]
        c_t, flip = ((1 - core, 0), (core, 1), (1 - core, 1))[n]
        x_t = (1 - x_lo) if flip else x_lo
        cols = lanes((2 * x_t + c_t) * 1024 + start, width)
        there = lanes(start, width)
        slot = 2 * flip + core
        return [
            remote(src.at[:, cols], dst.at[slot, :, there], ex_send.at[i, n, piece], ex_recv.at[i, n, piece], mates[n])
            for i, (src, dst) in enumerate(((q_in, q_s), (g_in, g_s)))
        ]

    ex = [[exchange(n, piece) for piece in range(3)] for n in range(3)]
    for n in (1, 2):
        for copy in ex[n][0]:
            copy.start()
    for piece in range(3):
        for copy in ex[0][piece]:
            copy.start()

    for i in range(2):
        for s in range(2):
            pltpu.make_async_copy(k_in, kv.at[i, s, y, z], a_recv.at[i, s]).wait()

    def y_of(g):
        base = y + (g // 2) * y_step
        return base + (g % 2) * (3 - 2 * base)

    def pair(g):
        return kv.at[:, :, y_of(g), z]

    y_copies = [
        remote(pair(g), pair(g), y_send.at[d], y_recv.at[d], y_all[to]) for d, (g, to) in enumerate(((0, 0), (0, 1), (1, 1)))
    ]
    z_sent = [
        [remote(pair(g), pair(g), z_send.at[g, d], z_recv.at[g, d], z_all[d]) for d in range(3)] for g in range(4)
    ]
    for copy in y_copies[:2] + z_sent[0]:
        copy.start()
    y_copies[0].wait()
    for peer in gate:
        pl.semaphore_signal(clear_sem, inc=1, device_id=peer, device_id_type=pl.DeviceIdType.MESH)
    for copy in [y_copies[2]] + z_sent[1]:
        copy.start()
    y_copies[1].wait_recv()
    for copy in z_sent[2]:
        copy.start()
    pl.semaphore_wait(clear_sem, 3)
    for piece in (1, 2):
        for n in (1, 2):
            for copy in ex[n][piece]:
                copy.start()
    y_copies[2].wait_recv()
    for copy in z_sent[3]:
        copy.start()
    for piece in range(3):
        for copy in ex[0][piece]:
            copy.wait_recv()
    lax.fori_loop(0, 4, lambda n, carry: prep((1 - core) * 4 + n), 0)

    def keys(i, kc):
        return kv[i, kc // 8, (kc // 2) % 4, pl.ds(2 * (kc % 2), 2)].reshape(CH, DH)

    def visible(pos, kc):
        key_pos = kc * CH + lax.broadcasted_iota(jnp.int32, (CH, 256), 0)
        query_pos = pos * TOK + (lax.broadcasted_iota(jnp.int32, (CH, 256), 1) & 127)
        return key_pos <= query_pos

    def stats(pos, kc, i, masked):
        cols = lanes(i * 256, 256)
        s = dot(keys(0, kc), q_t[:, cols])
        dp = dot(keys(1, kc), g_t[:, cols])
        if masked:
            s = jnp.where(visible(pos, kc), s, -1e30)
        s = s.reshape(CH // 8, 8, 256)
        dp = dp.reshape(CH // 8, 8, 256)
        old = m8[:, cols]
        new = jnp.maximum(old, jnp.max(s, axis=0))
        w = jnp.exp2((s - new) * EXPO)
        shrink = jnp.exp2((old - new) * EXPO)
        m8[:, cols] = new
        l8[:, cols] = l8[:, cols] * shrink + jnp.sum(w, axis=0)
        d8[:, cols] = d8[:, cols] * shrink + jnp.sum(w * dp, axis=0)

    def tile8(ref, s):
        return jnp.concatenate([ref[s, :, lanes(n * 128, 128)] for n in range(8)], axis=0)

    def grads(pos, kc, s, masked):
        at = (kc // 8, (kc // 2) % 4, pl.ds(2 * (kc % 2), 2))
        p_parts, ds_parts = [], []
        for n in range(4):
            cols = lanes(s * 1024 + n * 256, 256)
            scores = dot(keys(0, kc), q_t[:, cols])
            dp = dot(keys(1, kc), g_t[:, cols])
            p = jnp.exp2(scores * EXPO - top[:, cols])
            if masked:
                p = jnp.where(visible(pos, kc), p, 0.0)
            ds = p * (dp - rdot[:, cols])
            p_parts.append(p.astype(bf16))
            ds_parts.append(ds.astype(bf16))
        p_low, ds_low = jnp.concatenate(p_parts, axis=1), jnp.concatenate(ds_parts, axis=1)
        dkv[(1,) + at] += dot(p_low, tile8(g_s, s)).reshape(2, 128, 128)
        dkv[(0,) + at] += dot(ds_low, tile8(q_s, s)).reshape(2, 128, 128)
        acc[:, lanes(s * 1024, 1024)] += dot(k_t[:, lanes(kc * CH, CH)], ds_low)

    positions = (seq, 16 * (1 - x_lo) + 4 * (3 - y) + z)

    def chunk(fn, blk, kc, tiles):
        pos = positions[blk]

        @pl.when(kc < pos // 2)
        def _():
            for i in tiles:
                fn(pos, kc, i, False)

        @pl.when(kc == pos // 2)
        def _():
            for i in tiles:
                fn(pos, kc, i, True)

    def far_tiles(half):
        return [8 + 2 * half, 9 + 2 * half, 12 + 2 * half, 13 + 2 * half]

    def far_arrive(half):
        for n in (1, 2):
            for copy in ex[n][2] if half else ex[n][0] + ex[n][1]:
                copy.wait_recv()
        for i in far_tiles(half):
            prep(i)

    def first_rows(o, carry):
        g = o // 4

        @pl.when(o % 4 == 0)
        def _():
            for d in range(3):
                pltpu.make_async_copy(kv.at[:, :, 0, 0], kv.at[:, :, 0, 0], z_recv.at[g, d]).wait()

        @pl.when(o == 0)
        def _():
            far_arrive(0)

        kc = ((o // 2) % 2) * 8 + y_of(g) * 2 + o % 2
        k_t[:, lanes(kc * CH, CH)] = keys(0, kc).T
        chunk(stats, 0, kc, range(8))
        chunk(stats, 1, kc, far_tiles(0))
        return carry

    lax.fori_loop(0, 16, first_rows, 0)
    far_arrive(1)

    def last_rows(kc, carry):
        for i in far_tiles(1):
            stats(positions[1], kc, i, False)
        return carry

    lax.fori_loop(0, positions[1] // 2, last_rows, 0)
    for i in far_tiles(1):
        stats(positions[1], positions[1] // 2, i, True)

    high = jnp.max(m8[...], axis=0, keepdims=True)
    fold = jnp.exp2((m8[...] - high) * EXPO)
    total = jnp.sum(l8[...] * fold, axis=0, keepdims=True)
    top[...] = high * EXPO + jnp.log2(total)
    rdot[...] = jnp.sum(d8[...] * fold, axis=0, keepdims=True) / total

    z_spot = (z + 1 - 2 * (z % 2), (z + 2) % 4, 3 - z)
    z_peer = [dev(x_hi, core, x_lo, y, spot) for spot in z_spot]

    def term(g, spot):
        return dkv.at[:, :, y_of(g), spot]

    def z_copy(g, h, d):
        return remote(zst.at[g, d, :, h], zrc.at[g, d, :, h], zr_send.at[g, h, d], zr_recv.at[g, h, d], z_peer[d])

    zr_copies = [[z_copy(g, h, d) for h in range(2) for d in range(3)] for g in range(4)]
    f_copies = [remote(fst.at[n], frc.at[n], f_send.at[n], f_recv.at[n], y_all[1]) for n in range(2)]
    c_copy = remote(cst, crc, c_send, c_recv, y_all[0])

    def along_z(g, h, parts):
        for d in parts:
            zst[g, d, :, h] = dkv[:, h, y_of(g), z_spot[d]].astype(bf16)
            z_copy(g, h, d).start()

    def summed(g):
        for copy in zr_copies[g]:
            copy.wait_recv()
        return term(g, z)[...] + zrc[g, 0].astype(f32) + zrc[g, 1].astype(f32) + zrc[g, 2].astype(f32)

    def over_free(n):
        fst[n] = summed(3 - n).astype(bf16)
        f_copies[n].start()

    def over_cross():
        part = summed(1)
        f_copies[0].wait_recv()
        cst[...] = (part + frc[0].astype(f32)).astype(bf16)
        c_copy.start()

    def x_copies(h):
        to_self = jnp.logical_and(x_hi == x_lo, h == x_lo)
        local = pltpu.make_async_copy(fin.at[:, h], rcx.at[x_hi], x_recv.at[x_hi])
        away = remote(fin.at[:, h], rcx.at[x_hi], x_send.at[h], x_recv.at[x_hi], x_from(h))
        return to_self, local, away

    def along_x():
        part = summed(0)
        f_copies[1].wait_recv()
        c_copy.wait_recv()
        fin[...] = (part + frc[1].astype(f32) + crc[...].astype(f32)).astype(bf16)
        for h in range(2):
            to_self, local, away = x_copies(h)

            @pl.when(to_self)
            def _(local=local):
                local.start()

            @pl.when(jnp.logical_not(to_self))
            def _(away=away):
                away.start()

    def finish(s):
        for n in range(4):
            t = (acc[:, lanes((s * 4 + n) * 256, 256)] * SCALE).T.astype(bf16)
            dq_s[s, :, lanes(n * 256, 128)] = t[:128]
            dq_s[s, :, lanes(n * 256 + 128, 128)] = t[128:]

    back = [
        remote(dq_s.at[2 * flip + c_t], dq_out.at[:, own_cols], dq_send.at[n], dq_recv.at[n], mates[n])
        for n, (c_t, flip) in enumerate(((1 - core, 0), (core, 1), (1 - core, 1)))
    ]
    mine = pltpu.make_async_copy(dq_s.at[core], dq_out.at[:, own_cols], loc.at[2])
    def when(cond, *acts):
        @pl.when(cond)
        def _():
            for act in acts:
                act()

    def chunk_at(g, o):
        return (o // 2) * 8 + y_of(g) * 2 + (z // 2 + 1 + o) % 2

    def send_parts(g, o):
        for h in range(2):
            when(o == 2 * h, lambda: along_z(g, h, (1, 2)))
            when(o == 2 * h + 1, lambda: along_z(g, h, (0,)))

    def second_rows(o, carry):
        when(o == 10, lambda: over_free(0))
        for blk in range(2):
            chunk(grads, blk, chunk_at(3 - o // 4, o % 4), [2 * blk, 2 * blk + 1])
        send_parts(3 - o // 4, o % 4)
        return carry

    lax.fori_loop(0, 12, second_rows, 0)

    def third_rows(o, carry):
        when(o == 4, lambda: over_free(1))
        when(
            o == 4,
            lambda: finish(3 - core), lambda: back[2].start(),
            lambda: finish(1 - core), lambda: back[0].start(),
        )
        layer = (core + 1 + o // 4) % 2
        for blk in range(2):
            chunk(grads, blk, chunk_at(0, o % 4), [2 * blk + layer])
        send_parts(0, o - 4)
        return carry

    lax.fori_loop(0, 8, third_rows, 0)
    over_cross()
    finish(2 + core)
    back[1].start()
    finish(core)
    mine.start()
    along_x()

    for s in range(2):
        pltpu.make_async_copy(fin.at[:, 0], rcx.at[s], x_recv.at[s]).wait()
    total = rcx[0].astype(f32) + rcx[1].astype(f32)
    dk_out[...] = (total[0] * SCALE).astype(bf16)
    dv_out[...] = total[1].astype(bf16)

    mine.wait()
    for copy in back:
        copy.wait()
    for copy in sum(ex[0] + ex[1] + ex[2], []) + y_copies[1:] + sum(z_sent, []) + sum(zr_copies, []) + f_copies + [c_copy]:
        copy.wait_send()
    for t in range(2):
        to_self, pairs = a_copies(t)
        for _, away in pairs:
            @pl.when(jnp.logical_not(to_self))
            def _(away=away):
                away.wait_send()

        to_self, _, away = x_copies(t)

        @pl.when(jnp.logical_not(to_self))
        def _(away=away):
            away.wait_send()


def body(queries, shared_keys, shared_values, out_grad):
    any_, vmem = pl.BlockSpec(memory_space=pl.ANY), pl.BlockSpec(memory_space=pltpu.VMEM)
    dma = pltpu.SemaphoreType.DMA
    part = (2, 2, 128, 128)
    dq, dk, dv = pl.pallas_call(
        kernel,
        out_shape=(
            jax.ShapeDtypeStruct((128, 4096), bf16),
            jax.ShapeDtypeStruct((128, 128), bf16),
            jax.ShapeDtypeStruct((128, 128), bf16),
        ),
        in_specs=[any_] * 4,
        out_specs=(any_, vmem, vmem),
        scratch_shapes=[
            pltpu.VMEM((4, 128, 1024), bf16),
            pltpu.VMEM((4, 128, 1024), bf16),
            pltpu.VMEM((4, 128, 1024), bf16),
            pltpu.VMEM((2, 2, 4, 4, 128, 128), bf16),
            pltpu.VMEM((128, 4096), bf16),
            pltpu.VMEM((128, 4096), bf16),
            pltpu.VMEM((128, 4096), bf16),
            pltpu.VMEM((128, 4096), f32),
            pltpu.VMEM((2, 2, 4, 4, 128, 128), f32),
            pltpu.VMEM((8, 4096), f32),
            pltpu.VMEM((8, 4096), f32),
            pltpu.VMEM((8, 4096), f32),
            pltpu.VMEM((1, 4096), f32),
            pltpu.VMEM((1, 4096), f32),
            pltpu.VMEM((4, 3) + part, bf16),
            pltpu.VMEM((4, 3) + part, bf16),
            pltpu.VMEM((2,) + part, bf16),
            pltpu.VMEM((2,) + part, bf16),
            pltpu.VMEM(part, bf16),
            pltpu.VMEM(part, bf16),
            pltpu.VMEM(part, bf16),
            pltpu.VMEM(part, bf16),
            dma((2, 3, 3)), dma((2, 3, 3)), dma((3,)),
            dma((2, 2)), dma((2, 2)),
            pltpu.SemaphoreType.REGULAR,
            dma((3,)), dma((3,)), dma((4, 3)), dma((4, 3)),
            dma((4, 2, 3)), dma((4, 2, 3)), dma((2,)), dma((2,)), dma, dma,
            dma((2,)), dma((2,)),
            dma((3,)), dma((3,)),
        ],
        compiler_params=pltpu.CompilerParams(
            collective_id=0, has_side_effects=True, vmem_limit_bytes=56 * 2**20
        ),
        cost_estimate=pl.CostEstimate(flops=16 * 10**9, bytes_accessed=4 * 2**20, transcendentals=18 * 10**6),
    )(queries[0], shared_keys, shared_values, out_grad[0])
    return dq[None], dk, dv


def solution(mesh):
    return jax.shard_map(
        body,
        mesh=mesh,
        in_specs=(P("pipe", "seq", None), P("seq", "pipe"), P("seq", "pipe"), P("pipe", "seq", None)),
        out_specs=(P("pipe", "seq", None), P("seq", "pipe"), P("seq", "pipe")),
        check_vma=False,
    )
```

```python
import functools
import math

import jax
import jax.numpy as jnp
from jax import lax
from jax.experimental import pallas as pl
from jax.experimental.pallas import tpu as pltpu
from jax.sharding import PartitionSpec as P

DH = 128
TOK = 128
CH = 256
SCALE = 1.0 / math.sqrt(DH)
EXPO = math.log2(math.e) / math.sqrt(DH)
f32, bf16 = jnp.float32, jnp.bfloat16
NN = (((1,), (0,)), ((), ()))


def dot(a, b):
    return lax.dot_general(a, b, NN, preferred_element_type=f32)


def lanes(start, size):
    return pl.ds(pl.multiple_of(start, 128), size)


def kernel(
    q_in, k_in, v_in, g_in,
    dq_out, dk_out, dv_out,
    q_s, g_s, dq_s, kv, q_t, g_t, k_t, acc, dkv,
    m8, l8, d8, top, rdot,
    zst, zrc, fst, frc, cst, crc, fin, rcx,
    ex_send, ex_recv, loc, a_send, a_recv, clear_sem, y_send, y_recv, z_send, z_recv,
    zr_send, zr_recv, f_send, f_recv, c_send, c_recv, x_send, x_recv, dq_send, dq_recv,
):
    pipe = lax.axis_index("pipe")
    seq = lax.axis_index("seq")
    x_hi, core = pipe // 2, pipe % 2
    x_lo, y, z = seq // 16, (seq // 4) % 4, seq % 4
    head = 2 * x_lo + core

    def dev(x_hi_, core_, x_lo_, y_, z_):
        return {"pipe": x_hi_ * 2 + core_, "seq": x_lo_ * 16 + y_ * 4 + z_}

    def remote(src, dst, send, recv, to):
        return pltpu.make_async_remote_copy(
            src_ref=src, dst_ref=dst, send_sem=send, recv_sem=recv,
            device_id=to, device_id_type=pl.DeviceIdType.MESH,
        )

    mates = [
        dev(x_hi, 1 - core, x_lo, y, z),
        dev(x_hi, core, 1 - x_lo, 3 - y, z),
        dev(x_hi, 1 - core, 1 - x_lo, 3 - y, z),
    ]
    y_up, y_dn = dev(x_hi, core, x_lo, (y + 1) % 4, z), dev(x_hi, core, x_lo, (y + 3) % 4, z)
    z_up, z_dn = dev(x_hi, core, x_lo, y, (z + 1) % 4), dev(x_hi, core, x_lo, y, (z + 3) % 4)
    y_step = 1 - 2 * (y % 2)
    y_all = (dev(x_hi, core, x_lo, 3 - y, z), dev(x_hi, core, x_lo, y + y_step, z))
    gate = [dev(x_hi, core, 1 - x_lo, y, z), dev(x_hi, 1 - core, 1 - x_lo, y, z)]
    z_all = (z_up, z_dn, dev(x_hi, core, x_lo, y, (z + 2) % 4))

    def x_to(t):
        return dev(t, core, x_hi, y, z)

    def x_from(s):
        return dev(x_lo, core, s, y, z)

    barrier = pltpu.get_barrier_semaphore()
    for peer in mates + list(y_all + z_all) + gate:
        pl.semaphore_signal(barrier, inc=1, device_id=peer, device_id_type=pl.DeviceIdType.MESH)
    for t in range(2):
        @pl.when(jnp.logical_not(jnp.logical_and(t == x_hi, x_lo == x_hi)))
        def _():
            pl.semaphore_signal(barrier, inc=1, device_id=x_to(t), device_id_type=pl.DeviceIdType.MESH)

        @pl.when(jnp.logical_not(jnp.logical_and(x_lo == x_hi, t == x_lo)))
        def _():
            pl.semaphore_signal(barrier, inc=1, device_id=x_from(t), device_id_type=pl.DeviceIdType.MESH)

    own_cols = lanes(head * 1024, 1024)
    own = [
        pltpu.make_async_copy(q_in.at[:, own_cols], q_s.at[core], loc.at[0]),
        pltpu.make_async_copy(g_in.at[:, own_cols], g_s.at[core], loc.at[1]),
    ]
    for copy in own:
        copy.start()

    def clear(i, carry):
        dkv[i // 8, (i // 4) % 2, i % 4] = jnp.zeros((4, 128, 128), f32)
        return carry

    lax.fori_loop(0, 16, clear, 0)
    acc[...] = jnp.zeros_like(acc)
    m8[...] = jnp.full_like(m8, -1e30)
    l8[...] = jnp.zeros_like(l8)
    d8[...] = jnp.zeros_like(d8)

    def tile2(ref, i):
        s, n = i // 4, i % 4
        return jnp.concatenate(
            [ref[s, :, lanes(n * 256, 128)], ref[s, :, lanes(n * 256 + 128, 128)]], axis=0
        )

    def prep(i, carry=0):
        cols = lanes(i * 256, 256)
        q_t[:, cols] = tile2(q_s, i).T
        g_t[:, cols] = tile2(g_s, i).T
        return carry

    for copy in own:
        copy.wait()
    lax.fori_loop(0, 4, lambda n, carry: prep(core * 4 + n), 0)

    @pl.when(x_hi == x_lo)
    def _():
        pl.semaphore_wait(barrier, 12)

    @pl.when(x_hi != x_lo)
    def _():
        pl.semaphore_wait(barrier, 14)

    def a_copies(t):
        to_self = jnp.logical_and(t == x_hi, x_lo == x_hi)
        pairs = []
        for i, src in enumerate((k_in, v_in)):
            dst = kv.at[i, x_lo, y, z]
            pairs.append((
                pltpu.make_async_copy(src, dst, a_recv.at[i, x_lo]),
                remote(src, dst, a_send.at[i, t], a_recv.at[i, x_lo], x_to(t)),
            ))
        return to_self, pairs

    for t in range(2):
        to_self, pairs = a_copies(t)
        for local, away in pairs:
            @pl.when(to_self)
            def _(local=local):
                local.start()

            @pl.when(jnp.logical_not(to_self))
            def _(away=away):
                away.start()

    def exchange(n, piece):
        start, width = ((0, 256), (256, 256), (512, 512))[piece]
        c_t, flip = ((1 - core, 0), (core, 1), (1 - core, 1))[n]
        x_t = (1 - x_lo) if flip else x_lo
        cols = lanes((2 * x_t + c_t) * 1024 + start, width)
        there = lanes(start, width)
        slot = 2 * flip + core
        return [
            remote(src.at[:, cols], dst.at[slot, :, there], ex_send.at[i, n, piece], ex_recv.at[i, n, piece], mates[n])
            for i, (src, dst) in enumerate(((q_in, q_s), (g_in, g_s)))
        ]

    ex = [[exchange(n, piece) for piece in range(3)] for n in range(3)]
    for n in (1, 2):
        for copy in ex[n][0]:
            copy.start()
    for piece in range(3):
        for copy in ex[0][piece]:
            copy.start()

    for i in range(2):
        for s in range(2):
            pltpu.make_async_copy(k_in, kv.at[i, s, y, z], a_recv.at[i, s]).wait()

    def y_of(g):
        base = y + (g // 2) * y_step
        return base + (g % 2) * (3 - 2 * base)

    def pair(g):
        return kv.at[:, :, y_of(g), z]

    y_copies = [
        remote(pair(g), pair(g), y_send.at[d], y_recv.at[d], y_all[to]) for d, (g, to) in enumerate(((0, 0), (0, 1), (1, 1)))
    ]
    z_sent = [
        [remote(pair(g), pair(g), z_send.at[g, d], z_recv.at[g, d], z_all[d]) for d in range(3)] for g in range(4)
    ]
    for copy in y_copies[:2] + z_sent[0]:
        copy.start()
    y_copies[0].wait()
    for peer in gate:
        pl.semaphore_signal(clear_sem, inc=1, device_id=peer, device_id_type=pl.DeviceIdType.MESH)
    for copy in [y_copies[2]] + z_sent[1]:
        copy.start()
    y_copies[1].wait_recv()
    for copy in z_sent[2]:
        copy.start()
    pl.semaphore_wait(clear_sem, 2)
    for piece in (1, 2):
        for n in (1, 2):
            for copy in ex[n][piece]:
                copy.start()
    y_copies[2].wait_recv()
    for copy in z_sent[3]:
        copy.start()
    for piece in range(3):
        for copy in ex[0][piece]:
            copy.wait_recv()
    lax.fori_loop(0, 4, lambda n, carry: prep((1 - core) * 4 + n), 0)

    def keys(i, kc):
        return kv[i, kc // 8, (kc // 2) % 4, pl.ds(2 * (kc % 2), 2)].reshape(CH, DH)

    def visible(pos, kc):
        key_pos = kc * CH + lax.broadcasted_iota(jnp.int32, (CH, 256), 0)
        query_pos = pos * TOK + (lax.broadcasted_iota(jnp.int32, (CH, 256), 1) & 127)
        return key_pos <= query_pos

    def stats(pos, kc, i, masked):
        cols = lanes(i * 256, 256)
        s = dot(keys(0, kc), q_t[:, cols])
        dp = dot(keys(1, kc), g_t[:, cols])
        if masked:
            s = jnp.where(visible(pos, kc), s, -1e30)
        s = s.reshape(CH // 8, 8, 256)
        dp = dp.reshape(CH // 8, 8, 256)
        old = m8[:, cols]
        new = jnp.maximum(old, jnp.max(s, axis=0))
        w = jnp.exp2((s - new) * EXPO)
        shrink = jnp.exp2((old - new) * EXPO)
        m8[:, cols] = new
        l8[:, cols] = l8[:, cols] * shrink + jnp.sum(w, axis=0)
        d8[:, cols] = d8[:, cols] * shrink + jnp.sum(w * dp, axis=0)

    def tile8(ref, s):
        return jnp.concatenate([ref[s, :, lanes(n * 128, 128)] for n in range(8)], axis=0)

    def grads(pos, kc, s, masked):
        at = (kc // 8, (kc // 2) % 4, pl.ds(2 * (kc % 2), 2))
        p_parts, ds_parts = [], []
        for n in range(4):
            cols = lanes(s * 1024 + n * 256, 256)
            scores = dot(keys(0, kc), q_t[:, cols])
            dp = dot(keys(1, kc), g_t[:, cols])
            p = jnp.exp2(scores * EXPO - top[:, cols])
            if masked:
                p = jnp.where(visible(pos, kc), p, 0.0)
            ds = p * (dp - rdot[:, cols])
            p_parts.append(p.astype(bf16))
            ds_parts.append(ds.astype(bf16))
        p_low, ds_low = jnp.concatenate(p_parts, axis=1), jnp.concatenate(ds_parts, axis=1)
        dkv[(1,) + at] += dot(p_low, tile8(g_s, s)).reshape(2, 128, 128)
        dkv[(0,) + at] += dot(ds_low, tile8(q_s, s)).reshape(2, 128, 128)
        acc[:, lanes(s * 1024, 1024)] += dot(k_t[:, lanes(kc * CH, CH)], ds_low)

    positions = (seq, 16 * (1 - x_lo) + 4 * (3 - y) + z)

    def chunk(fn, blk, kc, tiles):
        pos = positions[blk]

        @pl.when(kc < pos // 2)
        def _():
            for i in tiles:
                fn(pos, kc, i, False)

        @pl.when(kc == pos // 2)
        def _():
            for i in tiles:
                fn(pos, kc, i, True)

    def far_tiles(half):
        return [8 + 2 * half, 9 + 2 * half, 12 + 2 * half, 13 + 2 * half]

    def far_arrive(half):
        for n in (1, 2):
            for copy in ex[n][2] if half else ex[n][0] + ex[n][1]:
                copy.wait_recv()
        for i in far_tiles(half):
            prep(i)

    def first_rows(o, carry):
        g = o // 4

        @pl.when(o % 4 == 0)
        def _():
            for d in range(3):
                pltpu.make_async_copy(kv.at[:, :, 0, 0], kv.at[:, :, 0, 0], z_recv.at[g, d]).wait()

        @pl.when(o == 0)
        def _():
            far_arrive(0)

        kc = ((o // 2) % 2) * 8 + y_of(g) * 2 + o % 2
        k_t[:, lanes(kc * CH, CH)] = keys(0, kc).T
        chunk(stats, 0, kc, range(8))
        chunk(stats, 1, kc, far_tiles(0))
        return carry

    lax.fori_loop(0, 16, first_rows, 0)
    far_arrive(1)

    def last_rows(kc, carry):
        for i in far_tiles(1):
            stats(positions[1], kc, i, False)
        return carry

    lax.fori_loop(0, positions[1] // 2, last_rows, 0)
    for i in far_tiles(1):
        stats(positions[1], positions[1] // 2, i, True)

    high = jnp.max(m8[...], axis=0, keepdims=True)
    fold = jnp.exp2((m8[...] - high) * EXPO)
    total = jnp.sum(l8[...] * fold, axis=0, keepdims=True)
    top[...] = high * EXPO + jnp.log2(total)
    rdot[...] = jnp.sum(d8[...] * fold, axis=0, keepdims=True) / total

    z_spot = (z + 1 - 2 * (z % 2), (z + 2) % 4, 3 - z)
    z_peer = [dev(x_hi, core, x_lo, y, spot) for spot in z_spot]

    def term(g, spot):
        return dkv.at[:, :, y_of(g), spot]

    def z_copy(g, h, d):
        return remote(zst.at[g, d, :, h], zrc.at[g, d, :, h], zr_send.at[g, h, d], zr_recv.at[g, h, d], z_peer[d])

    zr_copies = [[z_copy(g, h, d) for h in range(2) for d in range(3)] for g in range(4)]
    f_copies = [remote(fst.at[n], frc.at[n], f_send.at[n], f_recv.at[n], y_all[1]) for n in range(2)]
    c_copy = remote(cst, crc, c_send, c_recv, y_all[0])

    def along_z(g, h, parts):
        for d in parts:
            zst[g, d, :, h] = dkv[:, h, y_of(g), z_spot[d]].astype(bf16)
            z_copy(g, h, d).start()

    def summed(g):
        for copy in zr_copies[g]:
            copy.wait_recv()
        return term(g, z)[...] + zrc[g, 0].astype(f32) + zrc[g, 1].astype(f32) + zrc[g, 2].astype(f32)

    def over_free(n):
        fst[n] = summed(3 - n).astype(bf16)
        f_copies[n].start()

    def over_cross():
        part = summed(1)
        f_copies[0].wait_recv()
        cst[...] = (part + frc[0].astype(f32)).astype(bf16)
        c_copy.start()

    def x_copies(h):
        to_self = jnp.logical_and(x_hi == x_lo, h == x_lo)
        local = pltpu.make_async_copy(fin.at[:, h], rcx.at[x_hi], x_recv.at[x_hi])
        away = remote(fin.at[:, h], rcx.at[x_hi], x_send.at[h], x_recv.at[x_hi], x_from(h))
        return to_self, local, away

    def along_x():
        part = summed(0)
        f_copies[1].wait_recv()
        c_copy.wait_recv()
        fin[...] = (part + frc[1].astype(f32) + crc[...].astype(f32)).astype(bf16)
        for h in range(2):
            to_self, local, away = x_copies(h)

            @pl.when(to_self)
            def _(local=local):
                local.start()

            @pl.when(jnp.logical_not(to_self))
            def _(away=away):
                away.start()

    def finish(s):
        for n in range(4):
            t = (acc[:, lanes((s * 4 + n) * 256, 256)] * SCALE).T.astype(bf16)
            dq_s[s, :, lanes(n * 256, 128)] = t[:128]
            dq_s[s, :, lanes(n * 256 + 128, 128)] = t[128:]

    back = [
        remote(dq_s.at[2 * flip + c_t], dq_out.at[:, own_cols], dq_send.at[n], dq_recv.at[n], mates[n])
        for n, (c_t, flip) in enumerate(((1 - core, 0), (core, 1), (1 - core, 1)))
    ]
    mine = pltpu.make_async_copy(dq_s.at[core], dq_out.at[:, own_cols], loc.at[2])
    def when(cond, *acts):
        @pl.when(cond)
        def _():
            for act in acts:
                act()

    def chunk_at(g, o):
        return (o // 2) * 8 + y_of(g) * 2 + (z // 2 + 1 + o) % 2

    def send_parts(g, o):
        for h in range(2):
            when(o == 2 * h, lambda: along_z(g, h, (1, 2)))
            when(o == 2 * h + 1, lambda: along_z(g, h, (0,)))

    def second_rows(o, carry):
        when(o == 10, lambda: over_free(0))
        for blk in range(2):
            chunk(grads, blk, chunk_at(3 - o // 4, o % 4), [2 * blk, 2 * blk + 1])
        send_parts(3 - o // 4, o % 4)
        return carry

    lax.fori_loop(0, 12, second_rows, 0)

    def third_rows(o, carry):
        when(o == 4, lambda: over_free(1))
        when(o == 7, over_cross)
        when(
            o == 4,
            lambda: finish(3 - core), lambda: back[2].start(),
            lambda: finish(1 - core), lambda: back[0].start(),
        )
        layer = (core + 1 + o // 4) % 2
        for blk in range(2):
            chunk(grads, blk, chunk_at(0, o % 4), [2 * blk + layer])
        send_parts(0, o - 4)
        return carry

    lax.fori_loop(0, 8, third_rows, 0)
    finish(2 + core)
    back[1].start()
    finish(core)
    mine.start()
    along_x()

    for s in range(2):
        pltpu.make_async_copy(fin.at[:, 0], rcx.at[s], x_recv.at[s]).wait()
    total = rcx[0].astype(f32) + rcx[1].astype(f32)
    dk_out[...] = (total[0] * SCALE).astype(bf16)
    dv_out[...] = total[1].astype(bf16)

    mine.wait()
    for copy in back:
        copy.wait()
    for copy in sum(ex[0] + ex[1] + ex[2], []) + y_copies[1:] + sum(z_sent, []) + sum(zr_copies, []) + f_copies + [c_copy]:
        copy.wait_send()
    for t in range(2):
        to_self, pairs = a_copies(t)
        for _, away in pairs:
            @pl.when(jnp.logical_not(to_self))
            def _(away=away):
                away.wait_send()

        to_self, _, away = x_copies(t)

        @pl.when(jnp.logical_not(to_self))
        def _(away=away):
            away.wait_send()


def body(queries, shared_keys, shared_values, out_grad):
    any_, vmem = pl.BlockSpec(memory_space=pl.ANY), pl.BlockSpec(memory_space=pltpu.VMEM)
    dma = pltpu.SemaphoreType.DMA
    part = (2, 2, 128, 128)
    dq, dk, dv = pl.pallas_call(
        kernel,
        out_shape=(
            jax.ShapeDtypeStruct((128, 4096), bf16),
            jax.ShapeDtypeStruct((128, 128), bf16),
            jax.ShapeDtypeStruct((128, 128), bf16),
        ),
        in_specs=[any_] * 4,
        out_specs=(any_, vmem, vmem),
        scratch_shapes=[
            pltpu.VMEM((4, 128, 1024), bf16),
            pltpu.VMEM((4, 128, 1024), bf16),
            pltpu.VMEM((4, 128, 1024), bf16),
            pltpu.VMEM((2, 2, 4, 4, 128, 128), bf16),
            pltpu.VMEM((128, 4096), bf16),
            pltpu.VMEM((128, 4096), bf16),
            pltpu.VMEM((128, 4096), bf16),
            pltpu.VMEM((128, 4096), f32),
            pltpu.VMEM((2, 2, 4, 4, 128, 128), f32),
            pltpu.VMEM((8, 4096), f32),
            pltpu.VMEM((8, 4096), f32),
            pltpu.VMEM((8, 4096), f32),
            pltpu.VMEM((1, 4096), f32),
            pltpu.VMEM((1, 4096), f32),
            pltpu.VMEM((4, 3) + part, bf16),
            pltpu.VMEM((4, 3) + part, bf16),
            pltpu.VMEM((2,) + part, bf16),
            pltpu.VMEM((2,) + part, bf16),
            pltpu.VMEM(part, bf16),
            pltpu.VMEM(part, bf16),
            pltpu.VMEM(part, bf16),
            pltpu.VMEM(part, bf16),
            dma((2, 3, 3)), dma((2, 3, 3)), dma((3,)),
            dma((2, 2)), dma((2, 2)),
            pltpu.SemaphoreType.REGULAR,
            dma((3,)), dma((3,)), dma((4, 3)), dma((4, 3)),
            dma((4, 2, 3)), dma((4, 2, 3)), dma((2,)), dma((2,)), dma, dma,
            dma((2,)), dma((2,)),
            dma((3,)), dma((3,)),
        ],
        compiler_params=pltpu.CompilerParams(
            collective_id=0, has_side_effects=True, vmem_limit_bytes=56 * 2**20
        ),
        cost_estimate=pl.CostEstimate(flops=16 * 10**9, bytes_accessed=4 * 2**20, transcendentals=18 * 10**6),
    )(queries[0], shared_keys, shared_values, out_grad[0])
    return dq[None], dk, dv


def solution(mesh):
    return jax.shard_map(
        body,
        mesh=mesh,
        in_specs=(P("pipe", "seq", None), P("seq", "pipe"), P("seq", "pipe"), P("pipe", "seq", None)),
        out_specs=(P("pipe", "seq", None), P("seq", "pipe"), P("seq", "pipe")),
        check_vma=False,
    )
```

```python
import functools
import math

import jax
import jax.numpy as jnp
from jax import lax
from jax.experimental import pallas as pl
from jax.experimental.pallas import tpu as pltpu
from jax.sharding import PartitionSpec as P

DH = 128
TOK = 128
CH = 256
SCALE = 1.0 / math.sqrt(DH)
EXPO = math.log2(math.e) / math.sqrt(DH)
f32, bf16 = jnp.float32, jnp.bfloat16
NN = (((1,), (0,)), ((), ()))


def dot(a, b):
    return lax.dot_general(a, b, NN, preferred_element_type=f32)


def lanes(start, size):
    return pl.ds(pl.multiple_of(start, 128), size)


def kernel(
    q_in, k_in, v_in, g_in,
    dq_out, dk_out, dv_out,
    q_s, g_s, dq_s, kv, q_t, g_t, k_t, acc, dkv,
    m8, l8, d8, top, rdot,
    zst, zrc, fst, frc, cst, crc, fin, rcx,
    ex_send, ex_recv, loc, a_send, a_recv, clear_sem, y_send, y_recv, z_send, z_recv,
    zr_send, zr_recv, f_send, f_recv, c_send, c_recv, x_send, x_recv, dq_send, dq_recv,
):
    pipe = lax.axis_index("pipe")
    seq = lax.axis_index("seq")
    x_hi, core = pipe // 2, pipe % 2
    x_lo, y, z = seq // 16, (seq // 4) % 4, seq % 4
    head = 2 * x_lo + core

    def dev(x_hi_, core_, x_lo_, y_, z_):
        return {"pipe": x_hi_ * 2 + core_, "seq": x_lo_ * 16 + y_ * 4 + z_}

    def remote(src, dst, send, recv, to):
        return pltpu.make_async_remote_copy(
            src_ref=src, dst_ref=dst, send_sem=send, recv_sem=recv,
            device_id=to, device_id_type=pl.DeviceIdType.MESH,
        )

    mates = [
        dev(x_hi, 1 - core, x_lo, y, z),
        dev(x_hi, core, 1 - x_lo, 3 - y, z),
        dev(x_hi, 1 - core, 1 - x_lo, 3 - y, z),
    ]
    y_up, y_dn = dev(x_hi, core, x_lo, (y + 1) % 4, z), dev(x_hi, core, x_lo, (y + 3) % 4, z)
    z_up, z_dn = dev(x_hi, core, x_lo, y, (z + 1) % 4), dev(x_hi, core, x_lo, y, (z + 3) % 4)
    y_step = 1 - 2 * (y % 2)
    y_all = (dev(x_hi, core, x_lo, 3 - y, z), dev(x_hi, core, x_lo, y + y_step, z))
    gate = [mates[0], dev(x_hi, core, 1 - x_lo, y, z), dev(x_hi, 1 - core, 1 - x_lo, y, z)]
    z_all = (z_up, z_dn, dev(x_hi, core, x_lo, y, (z + 2) % 4))

    def x_to(t):
        return dev(t, core, x_hi, y, z)

    def x_from(s):
        return dev(x_lo, core, s, y, z)

    barrier = pltpu.get_barrier_semaphore()
    for peer in mates + list(y_all + z_all) + gate[1:]:
        pl.semaphore_signal(barrier, inc=1, device_id=peer, device_id_type=pl.DeviceIdType.MESH)
    for t in range(2):
        @pl.when(jnp.logical_not(jnp.logical_and(t == x_hi, x_lo == x_hi)))
        def _():
            pl.semaphore_signal(barrier, inc=1, device_id=x_to(t), device_id_type=pl.DeviceIdType.MESH)

        @pl.when(jnp.logical_not(jnp.logical_and(x_lo == x_hi, t == x_lo)))
        def _():
            pl.semaphore_signal(barrier, inc=1, device_id=x_from(t), device_id_type=pl.DeviceIdType.MESH)

    own_cols = lanes(head * 1024, 1024)
    own = [
        pltpu.make_async_copy(q_in.at[:, own_cols], q_s.at[core], loc.at[0]),
        pltpu.make_async_copy(g_in.at[:, own_cols], g_s.at[core], loc.at[1]),
    ]
    for copy in own:
        copy.start()

    def clear(i, carry):
        dkv[i // 8, (i // 4) % 2, i % 4] = jnp.zeros((4, 128, 128), f32)
        return carry

    lax.fori_loop(0, 16, clear, 0)
    acc[...] = jnp.zeros_like(acc)
    m8[...] = jnp.full_like(m8, -1e30)
    l8[...] = jnp.zeros_like(l8)
    d8[...] = jnp.zeros_like(d8)

    def tile2(ref, i):
        s, n = i // 4, i % 4
        return jnp.concatenate(
            [ref[s, :, lanes(n * 256, 128)], ref[s, :, lanes(n * 256 + 128, 128)]], axis=0
        )

    def prep(i, carry=0):
        cols = lanes(i * 256, 256)
        q_t[:, cols] = tile2(q_s, i).T
        g_t[:, cols] = tile2(g_s, i).T
        return carry

    for copy in own:
        copy.wait()
    lax.fori_loop(0, 4, lambda n, carry: prep(core * 4 + n), 0)

    @pl.when(x_hi == x_lo)
    def _():
        pl.semaphore_wait(barrier, 12)

    @pl.when(x_hi != x_lo)
    def _():
        pl.semaphore_wait(barrier, 14)

    def a_copies(t):
        to_self = jnp.logical_and(t == x_hi, x_lo == x_hi)
        pairs = []
        for i, src in enumerate((k_in, v_in)):
            dst = kv.at[i, x_lo, y, z]
            pairs.append((
                pltpu.make_async_copy(src, dst, a_recv.at[i, x_lo]),
                remote(src, dst, a_send.at[i, t], a_recv.at[i, x_lo], x_to(t)),
            ))
        return to_self, pairs

    for t in range(2):
        to_self, pairs = a_copies(t)
        for local, away in pairs:
            @pl.when(to_self)
            def _(local=local):
                local.start()

            @pl.when(jnp.logical_not(to_self))
            def _(away=away):
                away.start()

    def exchange(n, piece):
        start, width = ((0, 128), (128, 384), (512, 512))[piece]
        c_t, flip = ((1 - core, 0), (core, 1), (1 - core, 1))[n]
        x_t = (1 - x_lo) if flip else x_lo
        cols = lanes((2 * x_t + c_t) * 1024 + start, width)
        there = lanes(start, width)
        slot = 2 * flip + core
        return [
            remote(src.at[:, cols], dst.at[slot, :, there], ex_send.at[i, n, piece], ex_recv.at[i, n, piece], mates[n])
            for i, (src, dst) in enumerate(((q_in, q_s), (g_in, g_s)))
        ]

    ex = [[exchange(n, piece) for piece in range(3)] for n in range(3)]
    for n in (1, 2):
        for copy in ex[n][0]:
            copy.start()
    for piece in range(3):
        for copy in ex[0][piece]:
            copy.start()

    for i in range(2):
        for s in range(2):
            pltpu.make_async_copy(k_in, kv.at[i, s, y, z], a_recv.at[i, s]).wait()

    def y_of(g):
        base = y + (g // 2) * y_step
        return base + (g % 2) * (3 - 2 * base)

    def pair(g):
        return kv.at[:, :, y_of(g), z]

    y_copies = [
        remote(pair(g), pair(g), y_send.at[d], y_recv.at[d], y_all[to]) for d, (g, to) in enumerate(((0, 0), (0, 1), (1, 1)))
    ]
    z_sent = [
        [remote(pair(g), pair(g), z_send.at[g, d], z_recv.at[g, d], z_all[d]) for d in range(3)] for g in range(4)
    ]
    for copy in y_copies[:2] + z_sent[0]:
        copy.start()
    y_copies[0].wait()
    for peer in gate:
        pl.semaphore_signal(clear_sem, inc=1, device_id=peer, device_id_type=pl.DeviceIdType.MESH)
    for copy in [y_copies[2]] + z_sent[1]:
        copy.start()
    y_copies[1].wait_recv()
    for copy in z_sent[2]:
        copy.start()
    pl.semaphore_wait(clear_sem, 3)
    for piece in (1, 2):
        for n in (1, 2):
            for copy in ex[n][piece]:
                copy.start()
    y_copies[2].wait_recv()
    for copy in z_sent[3]:
        copy.start()
    for piece in range(3):
        for copy in ex[0][piece]:
            copy.wait_recv()
    lax.fori_loop(0, 4, lambda n, carry: prep((1 - core) * 4 + n), 0)

    def keys(i, kc):
        return kv[i, kc // 8, (kc // 2) % 4, pl.ds(2 * (kc % 2), 2)].reshape(CH, DH)

    def visible(pos, kc):
        key_pos = kc * CH + lax.broadcasted_iota(jnp.int32, (CH, 256), 0)
        query_pos = pos * TOK + (lax.broadcasted_iota(jnp.int32, (CH, 256), 1) & 127)
        return key_pos <= query_pos

    def stats(pos, kc, i, masked):
        cols = lanes(i * 256, 256)
        s = dot(keys(0, kc), q_t[:, cols])
        dp = dot(keys(1, kc), g_t[:, cols])
        if masked:
            s = jnp.where(visible(pos, kc), s, -1e30)
        s = s.reshape(CH // 8, 8, 256)
        dp = dp.reshape(CH // 8, 8, 256)
        old = m8[:, cols]
        new = jnp.maximum(old, jnp.max(s, axis=0))
        w = jnp.exp2((s - new) * EXPO)
        shrink = jnp.exp2((old - new) * EXPO)
        m8[:, cols] = new
        l8[:, cols] = l8[:, cols] * shrink + jnp.sum(w, axis=0)
        d8[:, cols] = d8[:, cols] * shrink + jnp.sum(w * dp, axis=0)

    def tile8(ref, s):
        return jnp.concatenate([ref[s, :, lanes(n * 128, 128)] for n in range(8)], axis=0)

    def grads(pos, kc, s, masked):
        at = (kc // 8, (kc // 2) % 4, pl.ds(2 * (kc % 2), 2))
        p_parts, ds_parts = [], []
        for n in range(4):
            cols = lanes(s * 1024 + n * 256, 256)
            scores = dot(keys(0, kc), q_t[:, cols])
            dp = dot(keys(1, kc), g_t[:, cols])
            p = jnp.exp2(scores * EXPO - top[:, cols])
            if masked:
                p = jnp.where(visible(pos, kc), p, 0.0)
            ds = p * (dp - rdot[:, cols])
            p_parts.append(p.astype(bf16))
            ds_parts.append(ds.astype(bf16))
        p_low, ds_low = jnp.concatenate(p_parts, axis=1), jnp.concatenate(ds_parts, axis=1)
        dkv[(1,) + at] += dot(p_low, tile8(g_s, s)).reshape(2, 128, 128)
        dkv[(0,) + at] += dot(ds_low, tile8(q_s, s)).reshape(2, 128, 128)
        acc[:, lanes(s * 1024, 1024)] += dot(k_t[:, lanes(kc * CH, CH)], ds_low)

    positions = (seq, 16 * (1 - x_lo) + 4 * (3 - y) + z)

    def chunk(fn, blk, kc, tiles):
        pos = positions[blk]

        @pl.when(kc < pos // 2)
        def _():
            for i in tiles:
                fn(pos, kc, i, False)

        @pl.when(kc == pos // 2)
        def _():
            for i in tiles:
                fn(pos, kc, i, True)

    def far_tiles(half):
        return [8 + 2 * half, 9 + 2 * half, 12 + 2 * half, 13 + 2 * half]

    def far_arrive(half):
        for n in (1, 2):
            for copy in ex[n][2] if half else ex[n][0] + ex[n][1]:
                copy.wait_recv()
        for i in far_tiles(half):
            prep(i)

    def first_rows(o, carry):
        g = o // 4

        @pl.when(o % 4 == 0)
        def _():
            for d in range(3):
                pltpu.make_async_copy(kv.at[:, :, 0, 0], kv.at[:, :, 0, 0], z_recv.at[g, d]).wait()

        @pl.when(o == 0)
        def _():
            far_arrive(0)

        kc = ((o // 2) % 2) * 8 + y_of(g) * 2 + o % 2
        k_t[:, lanes(kc * CH, CH)] = keys(0, kc).T
        chunk(stats, 0, kc, range(8))
        chunk(stats, 1, kc, far_tiles(0))
        return carry

    lax.fori_loop(0, 16, first_rows, 0)
    far_arrive(1)

    def last_rows(kc, carry):
        for i in far_tiles(1):
            stats(positions[1], kc, i, False)
        return carry

    lax.fori_loop(0, positions[1] // 2, last_rows, 0)
    for i in far_tiles(1):
        stats(positions[1], positions[1] // 2, i, True)

    high = jnp.max(m8[...], axis=0, keepdims=True)
    fold = jnp.exp2((m8[...] - high) * EXPO)
    total = jnp.sum(l8[...] * fold, axis=0, keepdims=True)
    top[...] = high * EXPO + jnp.log2(total)
    rdot[...] = jnp.sum(d8[...] * fold, axis=0, keepdims=True) / total

    z_spot = (z + 1 - 2 * (z % 2), (z + 2) % 4, 3 - z)
    z_peer = [dev(x_hi, core, x_lo, y, spot) for spot in z_spot]

    def term(g, spot):
        return dkv.at[:, :, y_of(g), spot]

    def z_copy(g, h, d):
        return remote(zst.at[g, d, :, h], zrc.at[g, d, :, h], zr_send.at[g, h, d], zr_recv.at[g, h, d], z_peer[d])

    zr_copies = [[z_copy(g, h, d) for h in range(2) for d in range(3)] for g in range(4)]
    f_copies = [remote(fst.at[n], frc.at[n], f_send.at[n], f_recv.at[n], y_all[1]) for n in range(2)]
    c_copy = remote(cst, crc, c_send, c_recv, y_all[0])

    def along_z(g, h, parts):
        for d in parts:
            zst[g, d, :, h] = dkv[:, h, y_of(g), z_spot[d]].astype(bf16)
            z_copy(g, h, d).start()

    def summed(g):
        for copy in zr_copies[g]:
            copy.wait_recv()
        return term(g, z)[...] + zrc[g, 0].astype(f32) + zrc[g, 1].astype(f32) + zrc[g, 2].astype(f32)

    def over_free(n):
        fst[n] = summed(3 - n).astype(bf16)
        f_copies[n].start()

    def over_cross():
        part = summed(1)
        f_copies[0].wait_recv()
        cst[...] = (part + frc[0].astype(f32)).astype(bf16)
        c_copy.start()

    def x_copies(h):
        to_self = jnp.logical_and(x_hi == x_lo, h == x_lo)
        local = pltpu.make_async_copy(fin.at[:, h], rcx.at[x_hi], x_recv.at[x_hi])
        away = remote(fin.at[:, h], rcx.at[x_hi], x_send.at[h], x_recv.at[x_hi], x_from(h))
        return to_self, local, away

    def along_x():
        part = summed(0)
        f_copies[1].wait_recv()
        c_copy.wait_recv()
        fin[...] = (part + frc[1].astype(f32) + crc[...].astype(f32)).astype(bf16)
        for h in range(2):
            to_self, local, away = x_copies(h)

            @pl.when(to_self)
            def _(local=local):
                local.start()

            @pl.when(jnp.logical_not(to_self))
            def _(away=away):
                away.start()

    def finish(s):
        for n in range(4):
            t = (acc[:, lanes((s * 4 + n) * 256, 256)] * SCALE).T.astype(bf16)
            dq_s[s, :, lanes(n * 256, 128)] = t[:128]
            dq_s[s, :, lanes(n * 256 + 128, 128)] = t[128:]

    back = [
        remote(dq_s.at[2 * flip + c_t], dq_out.at[:, own_cols], dq_send.at[n], dq_recv.at[n], mates[n])
        for n, (c_t, flip) in enumerate(((1 - core, 0), (core, 1), (1 - core, 1)))
    ]
    mine = pltpu.make_async_copy(dq_s.at[core], dq_out.at[:, own_cols], loc.at[2])
    def when(cond, *acts):
        @pl.when(cond)
        def _():
            for act in acts:
                act()

    def chunk_at(g, o):
        return (o // 2) * 8 + y_of(g) * 2 + (z // 2 + 1 + o) % 2

    def send_parts(g, o):
        for h in range(2):
            when(o == 2 * h, lambda: along_z(g, h, (1, 2)))
            when(o == 2 * h + 1, lambda: along_z(g, h, (0,)))

    def second_rows(o, carry):
        for blk in range(2):
            chunk(grads, blk, chunk_at(3 - o // 4, o % 4), [2 * blk, 2 * blk + 1])
        send_parts(3 - o // 4, o % 4)
        return carry

    lax.fori_loop(0, 12, second_rows, 0)

    def third_rows(o, carry):
        when(o == 1, lambda: over_free(0))
        when(o == 6, lambda: over_free(1))
        when(
            o == 4,
            lambda: finish(3 - core), lambda: back[2].start(),
            lambda: finish(1 - core), lambda: back[0].start(),
        )
        layer = (core + 1 + o // 4) % 2
        for blk in range(2):
            chunk(grads, blk, chunk_at(0, o % 4), [2 * blk + layer])
        send_parts(0, o - 4)
        return carry

    lax.fori_loop(0, 8, third_rows, 0)
    over_cross()
    finish(2 + core)
    back[1].start()
    finish(core)
    mine.start()
    along_x()

    for s in range(2):
        pltpu.make_async_copy(fin.at[:, 0], rcx.at[s], x_recv.at[s]).wait()
    total = rcx[0].astype(f32) + rcx[1].astype(f32)
    dk_out[...] = (total[0] * SCALE).astype(bf16)
    dv_out[...] = total[1].astype(bf16)

    mine.wait()
    for copy in back:
        copy.wait()
    for copy in sum(ex[0] + ex[1] + ex[2], []) + y_copies[1:] + sum(z_sent, []) + sum(zr_copies, []) + f_copies + [c_copy]:
        copy.wait_send()
    for t in range(2):
        to_self, pairs = a_copies(t)
        for _, away in pairs:
            @pl.when(jnp.logical_not(to_self))
            def _(away=away):
                away.wait_send()

        to_self, _, away = x_copies(t)

        @pl.when(jnp.logical_not(to_self))
        def _(away=away):
            away.wait_send()


def body(queries, shared_keys, shared_values, out_grad):
    any_, vmem = pl.BlockSpec(memory_space=pl.ANY), pl.BlockSpec(memory_space=pltpu.VMEM)
    dma = pltpu.SemaphoreType.DMA
    part = (2, 2, 128, 128)
    dq, dk, dv = pl.pallas_call(
        kernel,
        out_shape=(
            jax.ShapeDtypeStruct((128, 4096), bf16),
            jax.ShapeDtypeStruct((128, 128), bf16),
            jax.ShapeDtypeStruct((128, 128), bf16),
        ),
        in_specs=[any_] * 4,
        out_specs=(any_, vmem, vmem),
        scratch_shapes=[
            pltpu.VMEM((4, 128, 1024), bf16),
            pltpu.VMEM((4, 128, 1024), bf16),
            pltpu.VMEM((4, 128, 1024), bf16),
            pltpu.VMEM((2, 2, 4, 4, 128, 128), bf16),
            pltpu.VMEM((128, 4096), bf16),
            pltpu.VMEM((128, 4096), bf16),
            pltpu.VMEM((128, 4096), bf16),
            pltpu.VMEM((128, 4096), f32),
            pltpu.VMEM((2, 2, 4, 4, 128, 128), f32),
            pltpu.VMEM((8, 4096), f32),
            pltpu.VMEM((8, 4096), f32),
            pltpu.VMEM((8, 4096), f32),
            pltpu.VMEM((1, 4096), f32),
            pltpu.VMEM((1, 4096), f32),
            pltpu.VMEM((4, 3) + part, bf16),
            pltpu.VMEM((4, 3) + part, bf16),
            pltpu.VMEM((2,) + part, bf16),
            pltpu.VMEM((2,) + part, bf16),
            pltpu.VMEM(part, bf16),
            pltpu.VMEM(part, bf16),
            pltpu.VMEM(part, bf16),
            pltpu.VMEM(part, bf16),
            dma((2, 3, 3)), dma((2, 3, 3)), dma((3,)),
            dma((2, 2)), dma((2, 2)),
            pltpu.SemaphoreType.REGULAR,
            dma((3,)), dma((3,)), dma((4, 3)), dma((4, 3)),
            dma((4, 2, 3)), dma((4, 2, 3)), dma((2,)), dma((2,)), dma, dma,
            dma((2,)), dma((2,)),
            dma((3,)), dma((3,)),
        ],
        compiler_params=pltpu.CompilerParams(
            collective_id=0, has_side_effects=True, vmem_limit_bytes=56 * 2**20
        ),
        cost_estimate=pl.CostEstimate(flops=16 * 10**9, bytes_accessed=4 * 2**20, transcendentals=18 * 10**6),
    )(queries[0], shared_keys, shared_values, out_grad[0])
    return dq[None], dk, dv


def solution(mesh):
    return jax.shard_map(
        body,
        mesh=mesh,
        in_specs=(P("pipe", "seq", None), P("seq", "pipe"), P("seq", "pipe"), P("pipe", "seq", None)),
        out_specs=(P("pipe", "seq", None), P("seq", "pipe"), P("seq", "pipe")),
        check_vma=False,
    )
```
